256 devices in a mesh: db: 16 (over y_lo, x, core), pb: 16 (over z, y_hi).
Axes of the slice: x: 4, y: 4 (y_hi: 2, y_lo: 2; y = y_hi * 2 + y_lo), z: 8, core: 2. Of those that a mesh axis runs over, the one named last changes fastest.
Arguments:
- queries: bfloat16 [512, 512, 1280], P(('db', 'pb')), may hold values from -4 to 4
- query_scale: bfloat16 [512, 512], P(('db', 'pb')), may hold values from 0.0099487305 to 0.049804688
- query_mask: int32 [512, 512], P(('db', 'pb')), may hold values 0 or 1
- query_len: int32 [512], P(('db', 'pb')), may hold values from 64 to 512
- targets: bfloat16 [2048, 128, 1280], P(('db', 'pb')), may hold values from -4 to 4
- target_scale: bfloat16 [2048, 128], P(('db', 'pb')), may hold values from 0.0099487305 to 0.049804688
- target_mask: int32 [2048, 128], P(('db', 'pb')), may hold values 0 or 1
- target_len: int32 [2048], P(('db', 'pb')), may hold values from 32 to 128
- hit_ids: int32 [512, 8], P(('db', 'pb')), may hold values from 0 to 2047, as said below
Outputs:
- band: float32 [2, 2048, 2, 640], P(None, ('db', 'pb'))
- rescore: float32 [512, 8], P(('db', 'pb'))
The draws below stay inside these ranges and needn't reach their ends.
Inputs may be any that keep to these rules, and one draw needn't show every extreme that they name: `hit_ids`: the hits of the query tiles of shard a * 16 + b name target blocks of shards a * 16 + e, e < 16. Over the hits of one shard's query tiles, at most 2 name target blocks of one such shard, and in every shard's list some shard is named exactly 2 times; hits may repeat.
All inputs are finite; a program needn't handle non-finite values. No bound on the sum of `query_mask` or of `target_mask` on one device may be relied on, other than what follows from the above.
Results may differ from the reference program's by a relative error of at most 0.00045.
Values may be sent and summed in bfloat16 or wider, within the bound.
A program may use at most 128 MiB of HBM per device.

```python
import math
import jax
import jax.numpy as jnp
from jax import lax

D = 1280
QLEN = 512
TLEN = 128
QPD = 2
TGT_DEV = 8
HITS = 8
CAP = 2
NQ = 512
NTGT = 2048
N_DB = 16
N_PB = 16


def draw_hit_ids(key, part):
    devices_all = N_DB * N_PB
    slot_count = QPD * HITS
    device_keys = jax.random.split(key, devices_all)

    def one_device(device_key, shard):
        key_heavy, key_others, key_order, key_local = jax.random.split(device_key, 4)
        heavy = jax.random.randint(key_heavy, (), 0, N_PB)
        others = (heavy + 1 + jax.random.permutation(key_others, N_PB - 1)) % N_PB
        position = jnp.arange(slot_count)
        rest = others[jnp.maximum(position - CAP, 0) % (N_PB - 1)]
        owners = jnp.where(position < CAP, heavy, rest)
        owners = owners[jax.random.permutation(key_order, slot_count)]
        local_ids = jax.random.randint(key_local, (slot_count,), 0, TGT_DEV)
        db_row = shard // N_PB
        return ((db_row * N_PB + owners) * TGT_DEV + local_ids).astype(jnp.int32).reshape(QPD, HITS)
    drawn = jax.vmap(one_device)(device_keys, jnp.arange(devices_all))
    return drawn.reshape(NQ, HITS)


def plant(result, rng, smallest, top_value):
    longest = result.shape.index(max(result.shape))
    spots = []
    for shift in (0, 1):
        where = [jax.random.randint(jax.random.fold_in(rng, axis), (), 0, length) for axis, length in enumerate(result.shape)]
        where[longest] = (where[longest] + shift) % result.shape[longest]
        spots.append(tuple(where))
    return result.at[spots[0]].set(smallest).at[spots[1]].set(top_value)


def levels(rng, shape, cuts, least, top_value):
    def one(dim, parts):
        steps = jax.random.uniform(jax.random.fold_in(jax.random.fold_in(rng, 6), dim), (parts,), jnp.float32, least / len(cuts), top_value / len(cuts))
        return jnp.repeat(jnp.exp(steps), shape[dim] // parts).reshape((-1,) + (1,) * (len(shape) - dim - 1))

    loudness = one(*cuts[0])
    for cut in cuts[1:]:
        loudness = loudness * one(*cut)
    return loudness


def noise(rng, extent, deviation, most, shards=(), held_as=jnp.bfloat16):
    values = jax.random.normal(rng, extent, jnp.float32) * deviation
    if len(shards) > 0:
        values = levels(rng, extent, shards, -0.22, 0.18) * values
    return jnp.clip(values, min=-most, max=most).astype(held_as)


def setup_inputs(seed: int = 0) -> dict:
    key_list = jax.random.split(jax.random.key(seed), 10)
    queries = noise(key_list[0], (NQ, QLEN, D), 1.0, 4.0, ((0, 256),))
    query_scale = jnp.clip(jnp.exp(math.log(0.049804688) - 1.61066415 * jax.random.uniform(key_list[1], (NQ, QLEN), jnp.float32) ** levels(key_list[1], (NQ, QLEN), ((0, 256),), -0.2, 0.2)), 0.0099487305, 0.049804688).astype(jnp.bfloat16)
    query_mask = plant((jax.random.randint(key_list[2], (NQ, QLEN), 0, 10) < 9).astype(jnp.int32), jax.random.fold_in(key_list[2], 1), 0, 1)
    query_len = plant(jax.random.randint(key_list[3], (NQ,), QLEN // 8, QLEN + 1), jax.random.fold_in(key_list[3], 1), QLEN // 8, QLEN).astype(jnp.int32)
    targets = noise(key_list[4], (NTGT, TLEN, D), 1.0, 4.0, ((0, 256),))
    target_scale = jnp.clip(jnp.exp(math.log(0.049804688) - 1.61066415 * jax.random.uniform(key_list[5], (NTGT, TLEN), jnp.float32) ** levels(key_list[5], (NTGT, TLEN), ((0, 256),), -0.2, 0.2)), 0.0099487305, 0.049804688).astype(jnp.bfloat16)
    target_mask = plant((jax.random.randint(key_list[6], (NTGT, TLEN), 0, 10) < 9).astype(jnp.int32), jax.random.fold_in(key_list[6], 1), 0, 1)
    target_len = plant(jax.random.randint(key_list[7], (NTGT,), TLEN // 4, TLEN + 1), jax.random.fold_in(key_list[7], 1), TLEN // 4, TLEN).astype(jnp.int32)
    hit_ids = draw_hit_ids(jax.random.fold_in(key_list[9], 71), 0)
    return {"queries": queries, "query_scale": query_scale, "query_mask": query_mask, "query_len": query_len, "targets": targets, "target_scale": target_scale, "target_mask": target_mask, "target_len": target_len, "hit_ids": hit_ids}


def weights_of(scale, mask, length):
    position = jnp.arange(scale.shape[1], dtype=jnp.int32)
    live = (mask == 1) & (position[None, :] < length[:, None])
    return jnp.where(live, scale, jnp.zeros_like(scale))


def diagonal_band(scores):
    leading = scores.shape[:-2]
    query_rows = scores.shape[-2]
    target_rows = scores.shape[-1]
    span_cols = query_rows + target_rows
    flipped = scores[..., ::-1]
    padded = jnp.pad(flipped, [(0, 0)] * (scores.ndim - 1) + [(0, query_rows + 1)])
    flattened = padded.reshape(leading + (query_rows * (span_cols + 1),))
    sheared = flattened[..., : query_rows * span_cols].reshape(leading + (query_rows, span_cols))
    diagonals = jnp.sum(sheared, axis=-2)
    shifted = jnp.pad(diagonals, [(0, 0)] * (diagonals.ndim - 1) + [(1, 0)])[..., :span_cols]
    return diagonals + shifted


def reference(queries, query_scale, query_mask, query_len, targets, target_scale, target_mask, target_len, hit_ids):
    query_weight = weights_of(query_scale, query_mask, query_len)
    target_weight = weights_of(target_scale, target_mask, target_len)

    def per_target(target_id):
        shard = target_id // TGT_DEV
        db_row = shard // N_PB
        pb_col = shard % N_PB
        target_block = lax.dynamic_index_in_dim(targets, target_id, 0, keepdims=False).astype(jnp.float32)
        target_w = lax.dynamic_index_in_dim(target_weight, target_id, 0, keepdims=False).astype(jnp.float32)
        results = []
        for stop_index in (1, 2):
            source = ((((db_row - stop_index) % N_DB) * N_PB + pb_col) * QPD).astype(jnp.int32)
            query_block = lax.dynamic_slice_in_dim(queries, source, QPD, 0).astype(jnp.float32)
            query_w = lax.dynamic_slice_in_dim(query_weight, source, QPD, 0).astype(jnp.float32)
            raw = jnp.einsum("kid,jd->kij", query_block, target_block)
            scaled = raw * query_w[:, :, None] * target_w[None, None, :]
            results.append(diagonal_band(scaled))
        return jnp.stack(results)

    band = lax.map(per_target, jnp.arange(NTGT, dtype=jnp.int32))
    band = jnp.transpose(band, (1, 0, 2, 3))

    def per_query(query_id):
        query_block = lax.dynamic_index_in_dim(queries, query_id, 0, keepdims=False).astype(jnp.float32)
        query_w = lax.dynamic_index_in_dim(query_weight, query_id, 0, keepdims=False).astype(jnp.float32)
        listed = lax.dynamic_index_in_dim(hit_ids, query_id, 0, keepdims=False)
        chosen = jnp.take(targets, listed, axis=0).astype(jnp.float32)
        chosen_w = jnp.take(target_weight, listed, axis=0).astype(jnp.float32)
        raw = jnp.einsum("id,hjd->hij", query_block, chosen)
        scaled = raw * query_w[None, :, None] * chosen_w[:, None, :]
        banded = diagonal_band(scaled)
        return jnp.sum(jnp.maximum(banded, 0.0), axis=-1) / (QLEN + TLEN)

    rescore = lax.map(per_query, jnp.arange(NQ, dtype=jnp.int32))
    return band, rescore
```

```python
import functools

import jax
import jax.numpy as jnp
from jax import lax
from jax.experimental import pallas as pl
from jax.experimental.pallas import tpu as pltpu
from jax.sharding import PartitionSpec as P

MESH = pl.DeviceIdType.MESH
LANES = 128
NZ = 8
PEERS = NZ - 1
CHUNKS = 4


def weights_of(scale, mask, length):
    position = jnp.arange(scale.shape[1], dtype=jnp.int32)
    live = (mask == 1) & (position[None, :] < length[:, None])
    return jnp.where(live, scale, jnp.zeros_like(scale)).astype(jnp.float32)


def kernel(
    q_hbm, t_hbm, wt_in, wq_in, h_in, band_ref, resc_ref,
    qin, tin, ts, tall, qs, qr, qb, wt, wq, wqs, hv, hs, qwb, qwbb, sbuf, psum, prec, bo,
    in_sem, own_sem, t_send, t_recv, q_send, q_recv, y_send, y_recv, s2_send, s2_recv, s1_send, s1_recv,
    w_send, w_recv, m_send, m_recv, p_send, p_recv,
):
    n_db = lax.axis_size("db")
    db = lax.axis_index("db")
    pb = lax.axis_index("pb")
    z = pb // 2
    yh = lax.rem(pb, 2)
    core = lax.rem(db, 2)
    mate = db + 1 - 2 * core
    depth = ts.shape[2]
    half = qs.shape[3]

    def zdev(k):
        return (db, k * 2 + yh)

    def step_of(j):
        near = j // 2 + 1
        return jnp.where(lax.rem(j, 2) == 0, near, NZ - near)

    def to(j):
        return lax.rem(z + step_of(j), NZ)

    def frm(j):
        return lax.rem(z - step_of(j) + NZ, NZ)

    y_dev = (db, pb + 1 - 2 * yh)
    core_dev = (mate, pb)

    def shifted(by):
        return (lax.rem(db + by + n_db, n_db), pb)

    def remote(src, dst, send, recv, dev):
        return pltpu.make_async_remote_copy(
            src_ref=src, dst_ref=dst, send_sem=send, recv_sem=recv, device_id=dev, device_id_type=MESH
        )

    t_loads = [pltpu.make_async_copy(t_hbm.at[b], tin.at[b], in_sem.at[b]) for b in range(8)]
    q_loads = [pltpu.make_async_copy(q_hbm.at[k], qin.at[k], in_sem.at[8 + k]) for k in range(2)]
    for copy in t_loads + q_loads:
        copy.start()

    barrier = pltpu.get_barrier_semaphore()

    def greet(j, _):
        pl.semaphore_signal(barrier, inc=1, device_id=zdev(frm(j)), device_id_type=MESH)
        return 0

    lax.fori_loop(0, PEERS, greet, 0)
    for dev in (y_dev, core_dev, shifted(-1), shifted(-2)):
        pl.semaphore_signal(barrier, inc=1, device_id=dev, device_id_type=MESH)
    pl.semaphore_wait(barrier, PEERS + 4)

    s2 = [remote(q_hbm.at[k], qb.at[1, k], s2_send.at[k], s2_recv.at[k], shifted(2)) for k in range(2)]
    s1_even = [remote(q_hbm.at[k], qb.at[0, k], s1_send.at[k], s1_recv.at[k], core_dev) for k in range(2)]
    s1_odd = [remote(qb.at[1, k], qb.at[0, k], s1_send.at[k], s1_recv.at[k], core_dev) for k in range(2)]
    for copy in s2:
        copy.start()

    @pl.when(core == 0)
    def _():
        for copy in s1_even:
            copy.start()

    shift_w = [
        remote(wq_in, wqs.at[0], m_send.at[0], m_recv.at[0], shifted(1)),
        remote(wq_in, wqs.at[1], m_send.at[1], m_recv.at[1], shifted(2)),
    ]
    for copy in shift_w:
        copy.start()

    def small(j):
        dev = zdev(to(j))
        return [
            remote(wt_in, wt.at[z], w_send.at[0, j], w_recv.at[0, j], dev),
            remote(wq_in, wq.at[z], w_send.at[1, j], w_recv.at[1, j], dev),
            remote(h_in, hv.at[z], w_send.at[2, j], w_recv.at[2, j], dev),
        ]

    def start_small(j, _):
        for copy in small(j):
            copy.start()
        return 0

    lax.fori_loop(0, PEERS, start_small, 0)
    own_small = [
        pltpu.make_async_copy(wt_in, wt.at[z], own_sem.at[0]),
        pltpu.make_async_copy(wq_in, wq.at[z], own_sem.at[1]),
        pltpu.make_async_copy(h_in, hv.at[z], own_sem.at[2]),
    ]
    for copy in own_small:
        copy.start()

    flip = (
        lax.broadcasted_iota(jnp.int32, (LANES, LANES), 0) + lax.broadcasted_iota(jnp.int32, (LANES, LANES), 1)
        == LANES - 1
    ).astype(jnp.float32).astype(jnp.bfloat16)

    def t_copy(g, j):
        k = to(j)
        return remote(
            ts.at[k, pl.ds(2 * g, 2)], tall.at[z, pl.ds(2 * g, 2)], t_send.at[g, j], t_recv.at[g, j], zdev(k)
        )

    for copy in t_loads:
        copy.wait()

    def send_targets(g, _):
        for b in range(2):
            turned = jnp.dot(tin[2 * g + b].T, flip, preferred_element_type=jnp.float32).astype(jnp.bfloat16)
            ts[:, 2 * g + b] = turned.reshape(NZ, depth, LANES)

        def go(j, _):
            t_copy(g, j).start()
            return 0

        lax.fori_loop(0, PEERS, go, 0)
        return 0

    lax.fori_loop(0, 4, send_targets, 0)
    own_t = pltpu.make_async_copy(ts.at[z], tall.at[z], own_sem.at[3])
    own_t.start()

    for copy in q_loads:
        copy.wait()

    def q_copy(c, j):
        k = to(j)
        return remote(qs.at[k, c], qr.at[z, c], q_send.at[c, j], q_recv.at[c, j], zdev(k))

    def start_chunk(c):
        def go(j, _):
            q_copy(c, j).start()
            return 0

        lax.fori_loop(0, PEERS, go, 0)

    def turn_queries(c, _):
        rows = pl.ds(pl.multiple_of(lax.rem(c, 2) * half, half), half)
        turned = qin[c // 2, rows, :].T
        qs[:, c] = turned.reshape(NZ, depth, half)

        @pl.when(c == 0)
        def _():
            start_chunk(0)

        return 0

    lax.fori_loop(0, CHUNKS, turn_queries, 0)
    own_q = pltpu.make_async_copy(qs.at[z], qr.at[z], own_sem.at[4])
    own_q.start()

    def wait_small(j, _):
        for copy in small(j):
            copy.wait()
        return 0

    lax.fori_loop(0, PEERS, wait_small, 0)
    for copy in own_small:
        copy.wait()
    to_scalars = pltpu.make_async_copy(hv, hs, own_sem.at[5])
    to_scalars.start()
    for copy in shift_w:
        copy.wait()
    y_small = remote(wt.at[pl.ds(0, NZ)], wt.at[pl.ds(NZ, NZ)], m_send.at[2], m_recv.at[2], y_dev)
    y_small.start()

    def spread(row):
        return jnp.broadcast_to(row, (LANES, LANES)).T

    def spread_all(i, _):
        for m in range(8):
            rows = pl.ds((m % 4) * LANES, LANES)
            qwb[2 * i + m // 4, rows, :] = spread(wq[i, m : m + 1, :])
        return 0

    lax.fori_loop(0, NZ, spread_all, 0)

    def spread_shift(i, _):
        for m in range(8):
            rows = pl.ds((m % 4) * LANES, LANES)
            qwbb[2 * i + m // 4, rows, :] = spread(wqs[i, m : m + 1, :])
        return 0

    lax.fori_loop(0, 2, spread_shift, 0)

    def y_copy(i, src):
        return remote(tall.at[src], tall.at[NZ + src], y_send.at[i], y_recv.at[i], y_dev)

    own_t.wait()
    y_copy(PEERS, z).start()

    def pass_on(j, _):
        for g in range(4):
            t_copy(g, j).wait_recv()
        y_copy(j, frm(j)).start()
        return 0

    lax.fori_loop(0, PEERS, pass_on, 0)
    start_chunk(1)

    low = lax.broadcasted_iota(jnp.int32, (LANES, LANES), 1) >= lax.broadcasted_iota(jnp.int32, (LANES, LANES), 0)

    def diagonals(x):
        y = pltpu.roll(x, 0, 1, stride=1, stride_axis=0)
        lower = jnp.where(low, y, 0.0).reshape(LANES // 8, 8, LANES)
        upper = jnp.where(low, 0.0, y).reshape(LANES // 8, 8, LANES)
        return jnp.sum(lower, axis=0), jnp.sum(upper, axis=0)

    def row_sum(v):
        return jnp.sum(v, axis=0, keepdims=True)

    for k in range(2):
        s2[k].wait_recv()

    @pl.when(core == 1)
    def _():
        for copy in s1_odd:
            copy.start()

    def bands(s, k):
        def pair(p, _):
            rhs = jnp.concatenate(
                [ts[:, 2 * p].reshape(NZ * depth, LANES), ts[:, 2 * p + 1].reshape(NZ * depth, LANES)], axis=1
            )
            sbuf[...] = jnp.dot(qb[s, k], rhs, preferred_element_type=jnp.float32)
            for u in range(2):
                w8 = wt_in[2 * p + u]
                wrow = jnp.broadcast_to(w8[None], (LANES // 8, 8, LANES)).reshape(LANES, LANES)
                row = (s * 8 + 2 * p + u) * 2 + k
                carry = jnp.zeros((8, LANES), jnp.float32)
                for m in range(4):
                    rows = pl.ds(m * LANES, LANES)
                    x = sbuf[rows, u * LANES : (u + 1) * LANES] * qwbb[2 * s + k, rows, :] * wrow
                    lower, upper = diagonals(x)
                    bo[m, pl.ds(row, 1), :] = row_sum(carry + lower)
                    carry = upper
                bo[4, pl.ds(row, 1), :] = row_sum(carry)
            return 0

        lax.fori_loop(0, 4, pair, 0)

    lax.fori_loop(0, 2, lambda k, c: (bands(1, k), c)[1], 0)
    for k in range(2):
        s1_even[k].wait_recv()
    lax.fori_loop(0, 2, lambda k, c: (bands(0, k), c)[1], 0)

    def scores(segments):
        g = jnp.concatenate(segments, axis=1)
        return g + pltpu.roll(g, 1, 1)

    band_ref[...] = scores([bo[m] for m in range(5)])

    own_q.wait()
    to_scalars.wait()
    y_small.wait()
    psum[...] = jnp.zeros_like(psum)

    def wait_y(j, _):
        y_copy(j, frm(j)).wait()
        return 0

    lax.fori_loop(0, PEERS, wait_y, 0)
    y_copy(PEERS, z).wait()

    def chunk(c, _):
        def arrived(j, _):
            q_copy(c, j).wait_recv()
            return 0

        lax.fori_loop(0, PEERS, arrived, 0)

        @pl.when(c < CHUNKS - 2)
        def _():
            start_chunk(c + 2)

        tile, part = c // 2, lax.rem(c, 2)
        first = pl.multiple_of(part * half, half)

        def query(zq, _):
            lhs = qr[zq, c].T
            for pair in range(4):
                where = []
                for u in range(2):
                    hit = hs[zq, tile, 2 * pair + u]
                    owner, block = hit // 8, lax.rem(hit, 8)
                    other = jnp.where(lax.rem(owner, 2) == yh, 0, NZ)
                    where.append((other + owner // 2, block))
                rhs = jnp.concatenate([tall[o, b] for o, b in where], axis=1)
                s = jnp.dot(lhs, rhs, preferred_element_type=jnp.float32)
                for u in range(2):
                    o, b = where[u]
                    wrow = jnp.broadcast_to(wt[o, b][None], (LANES // 8, 8, LANES)).reshape(LANES, LANES)
                    row = tile * 8 + 2 * pair + u
                    carry = jnp.zeros((8, LANES), jnp.float32)
                    for m in range(2):
                        weight = qwb[2 * zq + tile, pl.ds(first + m * LANES, LANES), :]
                        x = s[m * LANES : (m + 1) * LANES, u * LANES : (u + 1) * LANES] * weight * wrow
                        lower, upper = diagonals(x)
                        psum[zq, 2 * part + m, pl.ds(row, 1), :] += row_sum(carry + lower)
                        carry = upper
                    psum[zq, 2 * part + 2, pl.ds(row, 1), :] += row_sum(carry)
            return 0

        lax.fori_loop(0, NZ, query, 0)
        return 0

    lax.fori_loop(0, CHUNKS, chunk, 0)

    def p_copy(j):
        k = to(j)
        return remote(psum.at[k], prec.at[z], p_send.at[j], p_recv.at[j], zdev(k))

    def start_p(j, _):
        p_copy(j).start()
        return 0

    lax.fori_loop(0, PEERS, start_p, 0)
    prec[z] = psum[z]

    def sent(j, _):
        for g in range(4):
            t_copy(g, j).wait_send()
        for c in range(CHUNKS):
            q_copy(c, j).wait_send()
        return 0

    lax.fori_loop(0, PEERS, sent, 0)
    for k in range(2):
        s2[k].wait_send()
        s1_even[k].wait_send()

    def wait_p(j, _):
        p_copy(j).wait()
        return 0

    lax.fori_loop(0, PEERS, wait_p, 0)
    total = prec[0]
    for k in range(1, NZ):
        total = total + prec[k]
    b = scores([total[m] for m in range(5)])
    mean = jnp.sum(jnp.maximum(b, 0.0), axis=1, keepdims=True) / (5 * LANES)
    resc_ref[...] = jnp.broadcast_to(mean, resc_ref.shape)


def shards(queries, query_scale, query_mask, query_len, targets, target_scale, target_mask, target_len, hit_ids):
    tiles, rows, width = queries.shape
    blocks, cols, _ = targets.shape
    hits = hit_ids.shape[1]
    depth = width // NZ
    half = rows // 2
    wq = weights_of(query_scale, query_mask, query_len).reshape(tiles * rows // LANES, LANES)
    wt = weights_of(target_scale, target_mask, target_len)[:, ::-1]
    wt = jnp.broadcast_to(wt[:, None, :], (blocks, 8, cols))
    group = lax.axis_size("pb") * blocks
    listed = jnp.zeros((8, LANES), jnp.int32).at[:tiles, :hits].set(hit_ids % group)
    vmem = functools.partial(pltpu.VMEM)
    dma = pltpu.SemaphoreType.DMA
    bf, f32 = jnp.bfloat16, jnp.float32
    band, resc = pl.pallas_call(
        kernel,
        out_shape=(
            jax.ShapeDtypeStruct((2 * blocks * tiles, rows + cols), f32),
            jax.ShapeDtypeStruct((tiles * hits, LANES), f32),
        ),
        in_specs=[pl.BlockSpec(memory_space=pl.ANY)] * 2 + [pl.BlockSpec(memory_space=pltpu.VMEM)] * 3,
        out_specs=(pl.BlockSpec(memory_space=pltpu.VMEM),) * 2,
        scratch_shapes=[
            vmem((tiles, rows, width), bf),
            vmem((blocks, cols, width), bf),
            vmem((NZ, blocks, depth, cols), bf),
            vmem((2 * NZ, blocks, depth, cols), bf),
            vmem((NZ, CHUNKS, depth, half), bf),
            vmem((NZ, CHUNKS, depth, half), bf),
            vmem((2, tiles, rows, width), bf),
            vmem((2 * NZ, blocks, 8, cols), f32),
            vmem((NZ, 8, LANES), f32),
            vmem((2, 8, LANES), f32),
            vmem((NZ, 8, LANES), jnp.int32),
            pltpu.SMEM((NZ, 8, LANES), jnp.int32),
            vmem((NZ * tiles, rows, LANES), f32),
            vmem((2 * tiles, rows, LANES), f32),
            vmem((rows, 2 * LANES), f32),
            vmem((NZ, 5, tiles * hits, LANES), f32),
            vmem((NZ, 5, tiles * hits, LANES), f32),
            vmem((5, 2 * blocks * tiles, LANES), f32),
            dma((10,)),
            dma((6,)),
            dma((4, PEERS)), dma((4, PEERS)),
            dma((CHUNKS, PEERS)), dma((CHUNKS, PEERS)),
            dma((NZ,)), dma((NZ,)),
            dma((2,)), dma((2,)),
            dma((2,)), dma((2,)),
            dma((3, PEERS)), dma((3, PEERS)),
            dma((3,)), dma((3,)),
            dma((PEERS,)), dma((PEERS,)),
        ],
        compiler_params=pltpu.CompilerParams(
            collective_id=0, has_side_effects=True, vmem_limit_bytes=56 * 1024 * 1024
        ),
    )(queries, targets, wt, wq, listed)
    return band.reshape(2, blocks, tiles, rows + cols), resc[:, 0].reshape(tiles, hits)


def solution(mesh):
    in_specs = (
        P(("db", "pb"), None, None),
        P(("db", "pb"), None),
        P(("db", "pb"), None),
        P(("db", "pb")),
        P(("db", "pb"), None, None),
        P(("db", "pb"), None),
        P(("db", "pb"), None),
        P(("db", "pb")),
        P(("db", "pb"), None),
    )
    out_specs = (P(None, ("db", "pb"), None, None), P(("db", "pb"), None))
    return jax.shard_map(shards, mesh=mesh, in_specs=in_specs, out_specs=out_specs, check_vma=False)
```

```python
import jax
import jax.numpy as jnp
from jax import lax
from jax.experimental import pallas as pl
from jax.experimental.pallas import tpu as pltpu
from jax.sharding import PartitionSpec as P

MESH = pl.DeviceIdType.MESH
LANES = 128
NZ = 8
PEERS = NZ - 1
CHUNKS = 4


def kernel(
    q_hbm, qsc, qmk, qln, t_hbm, tsc, tmk, tln, h_in, band_ref, resc_ref,
    qin, tin, ts, tall, qs, qr, qb, wown, wp, wps, wt, hown, hv, hs, qwb, qwbb, sbuf, psum, prec, bo,
    in_sem, own_sem, t_send, t_recv, q_send, q_recv, y_send, y_recv, s2_send, s2_recv, s1_send, s1_recv,
    w_send, w_recv, m_send, m_recv, p_send, p_recv,
):
    n_db = lax.axis_size("db")
    db = lax.axis_index("db")
    pb = lax.axis_index("pb")
    z = pb // 2
    yh = lax.rem(pb, 2)
    core = lax.rem(db, 2)
    mate = db + 1 - 2 * core
    depth = ts.shape[2]
    half = qs.shape[3]

    def zdev(k):
        return (db, k * 2 + yh)

    def step_of(j):
        near = j // 2 + 1
        return jnp.where(lax.rem(j, 2) == 0, near, NZ - near)

    def to(j):
        return lax.rem(z + step_of(j), NZ)

    def frm(j):
        return lax.rem(z - step_of(j) + NZ, NZ)

    y_dev = (db, pb + 1 - 2 * yh)
    core_dev = (mate, pb)

    def shifted(by):
        return (lax.rem(db + by + n_db, n_db), pb)

    def remote(src, dst, send, recv, dev):
        return pltpu.make_async_remote_copy(
            src_ref=src, dst_ref=dst, send_sem=send, recv_sem=recv, device_id=dev, device_id_type=MESH
        )

    t_loads = [pltpu.make_async_copy(t_hbm.at[b], tin.at[b], in_sem.at[b]) for b in range(8)]
    q_loads = [pltpu.make_async_copy(q_hbm.at[k], qin.at[k], in_sem.at[8 + k]) for k in range(2)]
    for copy in t_loads + q_loads:
        copy.start()

    barrier = pltpu.get_barrier_semaphore()

    def greet(j, _):
        pl.semaphore_signal(barrier, inc=1, device_id=zdev(frm(j)), device_id_type=MESH)
        return 0

    lax.fori_loop(0, PEERS, greet, 0)
    for dev in (y_dev, core_dev, shifted(-1), shifted(-2)):
        pl.semaphore_signal(barrier, inc=1, device_id=dev, device_id_type=MESH)

    flip = (
        lax.broadcasted_iota(jnp.int32, (LANES, LANES), 0) + lax.broadcasted_iota(jnp.int32, (LANES, LANES), 1)
        == LANES - 1
    ).astype(jnp.float32).astype(jnp.bfloat16)
    position = lax.broadcasted_iota(jnp.int32, (8, LANES), 1)
    place = lax.broadcasted_iota(jnp.int32, (8, LANES), 0)
    lengths = jnp.zeros((8, LANES), jnp.int32)
    for b in range(8):
        lengths = jnp.where(place == b, tln[b], lengths)
    t_scale = tsc[...].astype(jnp.float32)
    t_weight = jnp.where(tmk[...] == 1, jnp.where(position < lengths, t_scale, 0.0), 0.0)
    t_weight = jnp.dot(t_weight.astype(jnp.bfloat16), flip, preferred_element_type=jnp.float32)
    q_scale = qsc[...].astype(jnp.float32)
    q_mask = qmk[...]
    q_rows = []
    for k in range(2):
        for m in range(4):
            cols = slice(m * LANES, (m + 1) * LANES)
            at = lax.broadcasted_iota(jnp.int32, (1, LANES), 1) + m * LANES
            kept = jnp.where(at < qln[k], q_scale[k : k + 1, cols], 0.0)
            q_rows.append(jnp.where(q_mask[k : k + 1, cols] == 1, kept, 0.0))
    wown[...] = jnp.concatenate([t_weight] + q_rows, axis=0).astype(jnp.bfloat16)
    hown[...] = jnp.zeros_like(hown)
    hown[0:2, 0:8] = h_in[...]

    def turn_targets(g):
        for b in range(2):
            turned = jnp.dot(tin[2 * g + b].T, flip, preferred_element_type=jnp.float32).astype(jnp.bfloat16)
            ts[:, 2 * g + b] = turned.reshape(NZ, depth, LANES)

    def t_copy(g, j):
        k = to(j)
        return remote(
            ts.at[k, pl.ds(2 * g, 2)], tall.at[z, pl.ds(2 * g, 2)], t_send.at[g, j], t_recv.at[g, j], zdev(k)
        )

    def start_targets(g):
        def go(j, _):
            t_copy(g, j).start()
            return 0

        lax.fori_loop(0, PEERS, go, 0)

    t_loads[0].wait()
    t_loads[1].wait()
    turn_targets(0)
    pl.semaphore_wait(barrier, PEERS + 4)
    start_targets(0)

    s2 = [remote(q_hbm.at[k], qb.at[1, k], s2_send.at[k], s2_recv.at[k], shifted(2)) for k in range(2)]
    s1_even = [remote(q_hbm.at[k], qb.at[0, k], s1_send.at[k], s1_recv.at[k], core_dev) for k in range(2)]
    s1_odd = [remote(qb.at[1, k], qb.at[0, k], s1_send.at[k], s1_recv.at[k], core_dev) for k in range(2)]
    for copy in s2:
        copy.start()

    @pl.when(core == 0)
    def _():
        for copy in s1_even:
            copy.start()

    shift_w = [remote(wown, wps.at[i], m_send.at[i], m_recv.at[i], shifted(i + 1)) for i in range(2)]
    for copy in shift_w:
        copy.start()

    def small(j):
        dev = zdev(to(j))
        return [
            remote(wown, wp.at[z], w_send.at[0, j], w_recv.at[0, j], dev),
            remote(hown, hv.at[z], w_send.at[1, j], w_recv.at[1, j], dev),
        ]

    def start_small(j, _):
        for copy in small(j):
            copy.start()
        return 0

    lax.fori_loop(0, PEERS, start_small, 0)
    own_small = [
        pltpu.make_async_copy(wown, wp.at[z], own_sem.at[0]),
        pltpu.make_async_copy(hown, hv.at[z], own_sem.at[1]),
    ]
    for copy in own_small:
        copy.start()

    for copy in t_loads[2:]:
        copy.wait()

    def send_targets(g, _):
        turn_targets(g)
        start_targets(g)
        return 0

    lax.fori_loop(1, 4, send_targets, 0)
    own_t = pltpu.make_async_copy(ts.at[z], tall.at[z], own_sem.at[3])
    own_t.start()

    for copy in q_loads:
        copy.wait()

    def q_copy(c, j):
        k = to(j)
        return remote(qs.at[k, c], qr.at[z, c], q_send.at[c, j], q_recv.at[c, j], zdev(k))

    def start_chunk(c):
        def go(j, _):
            q_copy(c, j).start()
            return 0

        lax.fori_loop(0, PEERS, go, 0)

    def turn_queries(c, _):
        rows = pl.ds(pl.multiple_of(lax.rem(c, 2) * half, half), half)
        turned = qin[c // 2, rows, :].T
        qs[:, c] = turned.reshape(NZ, depth, half)

        @pl.when(c == 0)
        def _():
            start_chunk(0)

        return 0

    lax.fori_loop(0, CHUNKS, turn_queries, 0)
    own_q = pltpu.make_async_copy(qs.at[z], qr.at[z], own_sem.at[4])
    own_q.start()

    def wait_small(j, _):
        for copy in small(j):
            copy.wait()
        return 0

    lax.fori_loop(0, PEERS, wait_small, 0)
    for copy in own_small:
        copy.wait()
    to_scalars = pltpu.make_async_copy(hv, hs, own_sem.at[5])
    to_scalars.start()
    for copy in shift_w:
        copy.wait()
    y_small = remote(wp.at[pl.ds(0, NZ)], wp.at[pl.ds(NZ, NZ)], m_send.at[2], m_recv.at[2], y_dev)
    y_small.start()

    def spread(row):
        return jnp.broadcast_to(row, (LANES, LANES)).T

    def spread_all(i, _):
        w = wp[i].astype(jnp.float32)
        for m in range(8):
            rows = pl.ds((m % 4) * LANES, LANES)
            qwb[2 * i + m // 4, rows, :] = spread(w[8 + m : 9 + m])
        return 0

    lax.fori_loop(0, NZ, spread_all, 0)

    def widen(o, _):
        w = wp[o].astype(jnp.float32)
        for b in range(8):
            wt[o, b] = jnp.broadcast_to(w[b : b + 1], (8, LANES))
        return 0

    lax.fori_loop(0, NZ, widen, 0)

    def spread_shift(i, _):
        w = wps[i].astype(jnp.float32)
        for m in range(8):
            rows = pl.ds((m % 4) * LANES, LANES)
            qwbb[2 * i + m // 4, rows, :] = spread(w[8 + m : 9 + m])
        return 0

    lax.fori_loop(0, 2, spread_shift, 0)

    def y_copy(i, src):
        return remote(tall.at[src], tall.at[NZ + src], y_send.at[i], y_recv.at[i], y_dev)

    own_t.wait()
    y_copy(PEERS, z).start()

    def pass_on(j, _):
        for g in range(4):
            t_copy(g, j).wait_recv()
        y_copy(j, frm(j)).start()
        return 0

    lax.fori_loop(0, PEERS, pass_on, 0)
    start_chunk(1)

    def chunk_arrived(c):
        def go(j, _):
            q_copy(c, j).wait_recv()
            return 0

        lax.fori_loop(0, PEERS, go, 0)

    chunk_arrived(0)
    start_chunk(2)

    low = lax.broadcasted_iota(jnp.int32, (LANES, LANES), 1) >= lax.broadcasted_iota(jnp.int32, (LANES, LANES), 0)

    def diagonals(x):
        y = pltpu.roll(x, 0, 1, stride=1, stride_axis=0)
        lower = jnp.where(low, y, 0.0).reshape(LANES // 8, 8, LANES)
        upper = jnp.where(low, 0.0, y).reshape(LANES // 8, 8, LANES)
        return jnp.sum(lower, axis=0), jnp.sum(upper, axis=0)

    def row_sum(v):
        return jnp.sum(v, axis=0, keepdims=True)

    for k in range(2):
        s2[k].wait_recv()

    @pl.when(core == 1)
    def _():
        for copy in s1_odd:
            copy.start()

    def bands(s, k):
        def pair(p, _):
            rhs = jnp.concatenate(
                [ts[:, 2 * p].reshape(NZ * depth, LANES), ts[:, 2 * p + 1].reshape(NZ * depth, LANES)], axis=1
            )
            sbuf[...] = jnp.dot(qb[s, k], rhs, preferred_element_type=jnp.float32)
            for u in range(2):
                w8 = wt[z, 2 * p + u]
                wrow = jnp.broadcast_to(w8[None], (LANES // 8, 8, LANES)).reshape(LANES, LANES)
                row = (s * 8 + 2 * p + u) * 2 + k
                carry = jnp.zeros((8, LANES), jnp.float32)
                for m in range(4):
                    rows = pl.ds(m * LANES, LANES)
                    x = sbuf[rows, u * LANES : (u + 1) * LANES] * qwbb[2 * s + k, rows, :] * wrow
                    lower, upper = diagonals(x)
                    bo[m, pl.ds(row, 1), :] = row_sum(carry + lower)
                    carry = upper
                bo[4, pl.ds(row, 1), :] = row_sum(carry)
            return 0

        lax.fori_loop(0, 4, pair, 0)

    lax.fori_loop(0, 2, lambda k, c: (bands(1, k), c)[1], 0)
    chunk_arrived(1)
    start_chunk(3)
    for k in range(2):
        s1_even[k].wait_recv()
    lax.fori_loop(0, 2, lambda k, c: (bands(0, k), c)[1], 0)

    def scores(segments):
        g = jnp.concatenate(segments, axis=1)
        return g + pltpu.roll(g, 1, 1)

    band = scores([bo[m] for m in range(5)])
    for s in range(2):
        for t in range(8):
            band_ref[s, t] = band[(s * 8 + t) * 2 : (s * 8 + t) * 2 + 2]

    own_q.wait()
    to_scalars.wait()
    y_small.wait()
    lax.fori_loop(NZ, 2 * NZ, widen, 0)
    psum[...] = jnp.zeros_like(psum)

    def wait_y(j, _):
        y_copy(j, frm(j)).wait()
        return 0

    lax.fori_loop(0, PEERS, wait_y, 0)
    y_copy(PEERS, z).wait()

    def p_copy(part, j):
        k = to(j)
        tile, seg, count = ((0, 0, 5), (1, 0, 2), (1, 2, 3))[part]
        return remote(
            psum.at[k, tile, pl.ds(seg, count)], prec.at[z, tile, pl.ds(seg, count)],
            p_send.at[part, j], p_recv.at[part, j], zdev(k),
        )

    def start_p(part):
        def go(j, _):
            p_copy(part, j).start()
            return 0

        lax.fori_loop(0, PEERS, go, 0)

    def chunk(c, _):
        @pl.when(c >= 2)
        def _():
            chunk_arrived(c)

        @pl.when(c == CHUNKS - 1)
        def _():
            start_p(0)
            start_p(1)

        tile, part = c // 2, lax.rem(c, 2)
        first = pl.multiple_of(part * half, half)

        def query(zq, _):
            lhs = qr[zq, c].T
            for pair in range(4):
                where = []
                for u in range(2):
                    hit = lax.rem(hs[zq, tile, 2 * pair + u], 2 * NZ * 8)
                    owner, block = hit // 8, lax.rem(hit, 8)
                    other = jnp.where(lax.rem(owner, 2) == yh, 0, NZ)
                    where.append((other + owner // 2, block))
                rhs = jnp.concatenate([tall[o, b] for o, b in where], axis=1)
                s = jnp.dot(lhs, rhs, preferred_element_type=jnp.float32)
                for u in range(2):
                    o, b = where[u]
                    wrow = jnp.broadcast_to(wt[o, b][None], (LANES // 8, 8, LANES)).reshape(LANES, LANES)
                    row = 2 * pair + u
                    carry = jnp.zeros((8, LANES), jnp.float32)
                    for m in range(2):
                        weight = qwb[2 * zq + tile, pl.ds(first + m * LANES, LANES), :]
                        x = s[m * LANES : (m + 1) * LANES, u * LANES : (u + 1) * LANES] * weight * wrow
                        lower, upper = diagonals(x)
                        psum[zq, tile, 2 * part + m, row : row + 1, :] += row_sum(carry + lower)
                        carry = upper
                    psum[zq, tile, 2 * part + 2, row : row + 1, :] += row_sum(carry)
            return 0

        lax.fori_loop(0, NZ, query, 0)
        return 0

    lax.fori_loop(0, CHUNKS, chunk, 0)

    start_p(2)
    prec[z] = psum[z]

    def sent(j, _):
        for g in range(4):
            t_copy(g, j).wait_send()
        for c in range(CHUNKS):
            q_copy(c, j).wait_send()
        return 0

    lax.fori_loop(0, PEERS, sent, 0)
    for k in range(2):
        s2[k].wait_send()
        s1_even[k].wait_send()

    def wait_p(j, _):
        for part in range(3):
            p_copy(part, j).wait()
        return 0

    lax.fori_loop(0, PEERS, wait_p, 0)
    total = prec[0]
    for k in range(1, NZ):
        total = total + prec[k]
    for tile in range(2):
        b = scores([total[tile, m] for m in range(5)])
        mean = jnp.sum(jnp.maximum(b, 0.0), axis=1, keepdims=True) / (5 * LANES)
        line = jnp.sum(jnp.where(position == place, jnp.broadcast_to(mean, (8, LANES)), 0.0), axis=0, keepdims=True)
        resc_ref[tile : tile + 1, :] = line[:, 0:8]


def shards(queries, query_scale, query_mask, query_len, targets, target_scale, target_mask, target_len, hit_ids):
    tiles, rows, width = queries.shape
    blocks, cols, _ = targets.shape
    hits = hit_ids.shape[1]
    depth = width // NZ
    half = rows // 2
    vmem = pltpu.VMEM
    one = (pl.ANY, vmem, vmem, pltpu.SMEM)
    spaces = one + one + (vmem,)
    dma = pltpu.SemaphoreType.DMA
    bf, f32 = jnp.bfloat16, jnp.float32
    band, resc = pl.pallas_call(
        kernel,
        out_shape=(
            jax.ShapeDtypeStruct((2, blocks, tiles, rows + cols), f32),
            jax.ShapeDtypeStruct((tiles, hits), f32),
        ),
        in_specs=[pl.BlockSpec(memory_space=m) for m in spaces],
        out_specs=(pl.BlockSpec(memory_space=pltpu.VMEM),) * 2,
        scratch_shapes=[
            vmem((tiles, rows, width), bf),
            vmem((blocks, cols, width), bf),
            vmem((NZ, blocks, depth, cols), bf),
            vmem((2 * NZ, blocks, depth, cols), bf),
            vmem((NZ, CHUNKS, depth, half), bf),
            vmem((NZ, CHUNKS, depth, half), bf),
            vmem((2, tiles, rows, width), bf),
            vmem((16, LANES), bf),
            vmem((2 * NZ, 16, LANES), bf),
            vmem((2, 16, LANES), bf),
            vmem((2 * NZ, blocks, 8, cols), f32),
            vmem((8, LANES), jnp.int32),
            vmem((NZ, 8, LANES), jnp.int32),
            pltpu.SMEM((NZ, 8, LANES), jnp.int32),
            vmem((NZ * tiles, rows, LANES), f32),
            vmem((2 * tiles, rows, LANES), f32),
            vmem((rows, 2 * LANES), f32),
            vmem((NZ, tiles, 5, hits, LANES), f32),
            vmem((NZ, tiles, 5, hits, LANES), f32),
            vmem((5, 2 * blocks * tiles, LANES), f32),
            dma((10,)),
            dma((6,)),
            dma((4, PEERS)), dma((4, PEERS)),
            dma((CHUNKS, PEERS)), dma((CHUNKS, PEERS)),
            dma((NZ,)), dma((NZ,)),
            dma((2,)), dma((2,)),
            dma((2,)), dma((2,)),
            dma((2, PEERS)), dma((2, PEERS)),
            dma((3,)), dma((3,)),
            dma((3, PEERS)), dma((3, PEERS)),
        ],
        compiler_params=pltpu.CompilerParams(
            collective_id=0, has_side_effects=True, vmem_limit_bytes=56 * 1024 * 1024
        ),
    )(queries, query_scale, query_mask, query_len, targets, target_scale, target_mask, target_len, hit_ids)
    return band, resc


def solution(mesh):
    in_specs = (
        P(("db", "pb"), None, None),
        P(("db", "pb"), None),
        P(("db", "pb"), None),
        P(("db", "pb")),
        P(("db", "pb"), None, None),
        P(("db", "pb"), None),
        P(("db", "pb"), None),
        P(("db", "pb")),
        P(("db", "pb"), None),
    )
    out_specs = (P(None, ("db", "pb"), None, None), P(("db", "pb"), None))
    return jax.shard_map(shards, mesh=mesh, in_specs=in_specs, out_specs=out_specs, check_vma=False)
```

```python
import jax
import jax.numpy as jnp
from jax import lax
from jax.experimental import pallas as pl
from jax.experimental.pallas import tpu as pltpu
from jax.sharding import PartitionSpec as P

MESH = pl.DeviceIdType.MESH
LANES = 128
NZ = 8
PEERS = NZ - 1
AHEAD = 4
CHUNKS = 4


def kernel(
    q_hbm, qsc, qmk, qln, t_hbm, tsc, tmk, tln, h_in, band_ref, resc_ref,
    qin, tin, ts, tall, qs, qr, qb, wown, wp, wps, wt, hown, hv, hs, qwb, qwbb, sbuf, psum, prec, bo, via,
    in_sem, own_sem, t_send, t_recv, q_send, q_recv, y_send, y_recv, s2_send, s2_recv, s1_send, s1_recv,
    w_send, w_recv, m_send, m_recv, p_send, p_recv, v_send, v_recv,
):
    n_db = lax.axis_size("db")
    db = lax.axis_index("db")
    pb = lax.axis_index("pb")
    z = pb // 2
    yh = lax.rem(pb, 2)
    core = lax.rem(db, 2)
    mate = db + 1 - 2 * core
    last_x = lax.rem(db, 8) >= 6
    first_x = lax.rem(db, 8) < 2
    depth = ts.shape[2]
    half = qs.shape[3]

    def zdev(k):
        return (db, k * 2 + yh)

    def step_of(j):
        near = j // 2 + 1
        return jnp.where(lax.rem(j, 2) == 0, near, NZ - near)

    def to(j):
        return lax.rem(z + step_of(j), NZ)

    def frm(j):
        return lax.rem(z - step_of(j) + NZ, NZ)

    y_dev = (db, pb + 1 - 2 * yh)
    core_dev = (mate, pb)

    def shifted(by):
        return (lax.rem(db + by + n_db, n_db), pb)

    def remote(src, dst, send, recv, dev):
        return pltpu.make_async_remote_copy(
            src_ref=src, dst_ref=dst, send_sem=send, recv_sem=recv, device_id=dev, device_id_type=MESH
        )

    t_loads = [pltpu.make_async_copy(t_hbm.at[b], tin.at[b], in_sem.at[b]) for b in range(8)]
    q_loads = [pltpu.make_async_copy(q_hbm.at[k], qin.at[k], in_sem.at[8 + k]) for k in range(2)]
    for copy in t_loads + q_loads:
        copy.start()

    barrier = pltpu.get_barrier_semaphore()

    def greet(j, _):
        pl.semaphore_signal(barrier, inc=1, device_id=zdev(frm(j)), device_id_type=MESH)
        return 0

    lax.fori_loop(0, PEERS, greet, 0)
    for dev in (y_dev, core_dev, shifted(-1), shifted(-2)):
        pl.semaphore_signal(barrier, inc=1, device_id=dev, device_id_type=MESH)

    @pl.when(last_x)
    def _():
        pl.semaphore_signal(barrier, inc=1, device_id=shifted(8), device_id_type=MESH)

    @pl.when(first_x)
    def _():
        pl.semaphore_signal(barrier, inc=1, device_id=shifted(-10), device_id_type=MESH)

    flip = (
        lax.broadcasted_iota(jnp.int32, (LANES, LANES), 0) + lax.broadcasted_iota(jnp.int32, (LANES, LANES), 1)
        == LANES - 1
    ).astype(jnp.float32).astype(jnp.bfloat16)
    position = lax.broadcasted_iota(jnp.int32, (8, LANES), 1)
    place = lax.broadcasted_iota(jnp.int32, (8, LANES), 0)
    lengths = jnp.zeros((8, LANES), jnp.int32)
    for b in range(8):
        lengths = jnp.where(place == b, tln[b], lengths)
    t_scale = tsc[...].astype(jnp.float32)
    t_weight = jnp.where(tmk[...] == 1, jnp.where(position < lengths, t_scale, 0.0), 0.0)
    t_weight = jnp.dot(t_weight.astype(jnp.bfloat16), flip, preferred_element_type=jnp.float32)
    q_scale = qsc[...].astype(jnp.float32)
    q_mask = qmk[...]
    q_rows = []
    for k in range(2):
        for m in range(4):
            cols = slice(m * LANES, (m + 1) * LANES)
            at = lax.broadcasted_iota(jnp.int32, (1, LANES), 1) + m * LANES
            kept = jnp.where(at < qln[k], q_scale[k : k + 1, cols], 0.0)
            q_rows.append(jnp.where(q_mask[k : k + 1, cols] == 1, kept, 0.0))
    wown[...] = jnp.concatenate([t_weight] + q_rows, axis=0).astype(jnp.bfloat16)
    hown[...] = jnp.zeros_like(hown)
    hown[0:2, 0:8] = h_in[...]

    def turn_targets(g):
        for b in range(2):
            turned = jnp.dot(tin[2 * g + b].T, flip, preferred_element_type=jnp.float32).astype(jnp.bfloat16)
            ts[:, 2 * g + b] = turned.reshape(NZ, depth, LANES)

    def t_copy(g, j):
        k = to(j)
        return remote(
            ts.at[k, pl.ds(2 * g, 2)], tall.at[z, pl.ds(2 * g, 2)], t_send.at[g, j], t_recv.at[g, j], zdev(k)
        )

    def start_targets(g):
        def go(j, _):
            t_copy(g, j).start()
            return 0

        lax.fori_loop(0, PEERS, go, 0)

    t_loads[0].wait()
    t_loads[1].wait()
    turn_targets(0)
    pl.semaphore_wait(barrier, PEERS + 4 + jnp.where(last_x, 2, 0))

    shift_w = [remote(wown, wps.at[i], m_send.at[i], m_recv.at[i], shifted(i + 1)) for i in range(2)]
    for copy in shift_w:
        copy.start()

    def small(j):
        dev = zdev(to(j))
        return [
            remote(wown, wp.at[z], w_send.at[0, j], w_recv.at[0, j], dev),
            remote(hown, hv.at[z], w_send.at[1, j], w_recv.at[1, j], dev),
        ]

    def start_small(j, _):
        for copy in small(j):
            copy.start()
        return 0

    lax.fori_loop(0, PEERS, start_small, 0)
    own_small = [
        pltpu.make_async_copy(wown, wp.at[z], own_sem.at[0]),
        pltpu.make_async_copy(hown, hv.at[z], own_sem.at[1]),
    ]
    for copy in own_small:
        copy.start()

    start_targets(0)

    s2 = [remote(q_hbm.at[k], qb.at[1, k], s2_send.at[k], s2_recv.at[k], shifted(2)) for k in range(2)]
    s1_even = [remote(q_hbm.at[k], qb.at[0, k], s1_send.at[k], s1_recv.at[k], core_dev) for k in range(2)]
    s1_odd = [remote(qb.at[1, k], qb.at[0, k], s1_send.at[k], s1_recv.at[k], core_dev) for k in range(2)]
    s2_first = remote(q_hbm.at[1], via, v_send.at[0], v_recv.at[0], shifted(8))
    s2_then = remote(via, qb.at[1, 1], s2_send.at[1], s2_recv.at[1], shifted(10))
    s2[0].start()

    @pl.when(last_x)
    def _():
        s2_first.start()

    @pl.when(jnp.logical_not(last_x))
    def _():
        s2[1].start()

    @pl.when(core == 0)
    def _():
        for copy in s1_even:
            copy.start()

    for copy in t_loads[2:]:
        copy.wait()

    def send_targets(g, _):
        turn_targets(g)

        @pl.when(g < AHEAD)
        def _():
            start_targets(g)

        return 0

    lax.fori_loop(1, 4, send_targets, 0)
    own_t = pltpu.make_async_copy(ts.at[z], tall.at[z], own_sem.at[3])
    own_t.start()

    for copy in q_loads:
        copy.wait()

    def q_copy(c, j):
        k = to(j)
        return remote(qs.at[k, c], qr.at[z, c], q_send.at[c, j], q_recv.at[c, j], zdev(k))

    def start_chunk(c):
        def go(j, _):
            q_copy(c, j).start()
            return 0

        lax.fori_loop(0, PEERS, go, 0)

    def turn_queries(c, _):
        rows = pl.ds(pl.multiple_of(lax.rem(c, 2) * half, half), half)
        turned = qin[c // 2, rows, :].T
        qs[:, c] = turned.reshape(NZ, depth, half)

        @pl.when(c + 4 < AHEAD)
        def _():
            start_chunk(c)

        return 0

    lax.fori_loop(0, CHUNKS, turn_queries, 0)
    own_q = pltpu.make_async_copy(qs.at[z], qr.at[z], own_sem.at[4])
    own_q.start()

    def y_copy(g, i, src):
        part = pl.ds(2 * g, 2)
        return remote(tall.at[src, part], tall.at[NZ + src, part], y_send.at[g, i], y_recv.at[g, i], y_dev)

    own_t.wait()

    def pass_on(g, _):
        y_copy(g, PEERS, z).start()

        def go(j, _):
            t_copy(g, j).wait_recv()
            y_copy(g, j, frm(j)).start()
            later = g + AHEAD

            @pl.when(later < 4)
            def _():
                t_copy(later, j).start()

            @pl.when(jnp.logical_and(later >= 4, later < 8))
            def _():
                q_copy(later - 4, j).start()

            return 0

        lax.fori_loop(0, PEERS, go, 0)

        @pl.when(jnp.logical_and(g == 0, last_x))
        def _():
            s2_first.wait()
            s2_then.start()

        return 0

    lax.fori_loop(0, 4, pass_on, 0)

    def wait_small(j, _):
        for copy in small(j):
            copy.wait()
        return 0

    lax.fori_loop(0, PEERS, wait_small, 0)
    for copy in own_small:
        copy.wait()
    to_scalars = pltpu.make_async_copy(hv, hs, own_sem.at[5])
    to_scalars.start()
    for copy in shift_w:
        copy.wait()
    y_small = remote(wp.at[pl.ds(0, NZ)], wp.at[pl.ds(NZ, NZ)], m_send.at[2], m_recv.at[2], y_dev)
    y_small.start()

    def spread(row):
        return jnp.broadcast_to(row, (LANES, LANES)).T

    def spread_all(i, _):
        w = wp[i].astype(jnp.float32)
        for m in range(8):
            rows = pl.ds((m % 4) * LANES, LANES)
            qwb[2 * i + m // 4, rows, :] = spread(w[8 + m : 9 + m])
        return 0

    lax.fori_loop(0, NZ, spread_all, 0)

    def widen(o, _):
        w = wp[o].astype(jnp.float32)
        for b in range(8):
            wt[o, b] = jnp.broadcast_to(w[b : b + 1], (8, LANES))
        return 0

    lax.fori_loop(0, NZ, widen, 0)

    def spread_shift(i, _):
        w = wps[i].astype(jnp.float32)
        for m in range(8):
            rows = pl.ds((m % 4) * LANES, LANES)
            qwbb[2 * i + m // 4, rows, :] = spread(w[8 + m : 9 + m])
        return 0

    lax.fori_loop(0, 2, spread_shift, 0)

    def chunk_arrived(c):
        def go(j, _):
            q_copy(c, j).wait_recv()
            later = c + AHEAD

            @pl.when(later < CHUNKS)
            def _():
                q_copy(later, j).start()

            return 0

        lax.fori_loop(0, PEERS, go, 0)

    chunk_arrived(0)

    low = lax.broadcasted_iota(jnp.int32, (LANES, LANES), 1) >= lax.broadcasted_iota(jnp.int32, (LANES, LANES), 0)

    def diagonals(x):
        y = pltpu.roll(x, 0, 1, stride=1, stride_axis=0)
        lower = jnp.where(low, y, 0.0).reshape(LANES // 8, 8, LANES)
        upper = jnp.where(low, 0.0, y).reshape(LANES // 8, 8, LANES)
        return jnp.sum(lower, axis=0), jnp.sum(upper, axis=0)

    def row_sum(v):
        return jnp.sum(v, axis=0, keepdims=True)

    for k in range(2):
        s2[k].wait_recv()

    @pl.when(core == 1)
    def _():
        for copy in s1_odd:
            copy.start()

    def bands(s, k):
        def pair(p, _):
            rhs = jnp.concatenate(
                [ts[:, 2 * p].reshape(NZ * depth, LANES), ts[:, 2 * p + 1].reshape(NZ * depth, LANES)], axis=1
            )
            sbuf[...] = jnp.dot(qb[s, k], rhs, preferred_element_type=jnp.float32)
            for u in range(2):
                w8 = wt[z, 2 * p + u]
                wrow = jnp.broadcast_to(w8[None], (LANES // 8, 8, LANES)).reshape(LANES, LANES)
                row = (s * 8 + 2 * p + u) * 2 + k
                carry = jnp.zeros((8, LANES), jnp.float32)
                for m in range(4):
                    rows = pl.ds(m * LANES, LANES)
                    x = sbuf[rows, u * LANES : (u + 1) * LANES] * qwbb[2 * s + k, rows, :] * wrow
                    lower, upper = diagonals(x)
                    bo[m, pl.ds(row, 1), :] = row_sum(carry + lower)
                    carry = upper
                bo[4, pl.ds(row, 1), :] = row_sum(carry)
            return 0

        lax.fori_loop(0, 4, pair, 0)

    lax.fori_loop(0, 2, lambda k, c: (bands(1, k), c)[1], 0)
    chunk_arrived(1)
    for k in range(2):
        s1_even[k].wait_recv()
    lax.fori_loop(0, 2, lambda k, c: (bands(0, k), c)[1], 0)

    def scores(segments):
        g = jnp.concatenate(segments, axis=1)
        return g + pltpu.roll(g, 1, 1)

    band = scores([bo[m] for m in range(5)])
    for s in range(2):
        for t in range(8):
            band_ref[s, t] = band[(s * 8 + t) * 2 : (s * 8 + t) * 2 + 2]

    own_q.wait()
    to_scalars.wait()
    y_small.wait()
    lax.fori_loop(NZ, 2 * NZ, widen, 0)
    psum[...] = jnp.zeros_like(psum)

    def wait_y(g, _):
        def go(j, _):
            y_copy(g, j, frm(j)).wait()
            return 0

        lax.fori_loop(0, PEERS, go, 0)
        y_copy(g, PEERS, z).wait()
        return 0

    lax.fori_loop(0, 4, wait_y, 0)

    def p_copy(part, j):
        k = to(j)
        tile, seg, count = ((0, 0, 5), (1, 0, 2), (1, 2, 3))[part]
        return remote(
            psum.at[k, tile, pl.ds(seg, count)], prec.at[z, tile, pl.ds(seg, count)],
            p_send.at[part, j], p_recv.at[part, j], zdev(k),
        )

    def start_p(part):
        def go(j, _):
            p_copy(part, j).start()
            return 0

        lax.fori_loop(0, PEERS, go, 0)

    def chunk(c, _):
        @pl.when(c >= 2)
        def _():
            chunk_arrived(c)

        @pl.when(c == CHUNKS - 1)
        def _():
            start_p(0)
            start_p(1)

        tile, part = c // 2, lax.rem(c, 2)
        first = pl.multiple_of(part * half, half)

        def query(zq, _):
            lhs = qr[zq, c].T
            for pair in range(4):
                where = []
                for u in range(2):
                    hit = lax.rem(hs[zq, tile, 2 * pair + u], 2 * NZ * 8)
                    owner, block = hit // 8, lax.rem(hit, 8)
                    other = jnp.where(lax.rem(owner, 2) == yh, 0, NZ)
                    where.append((other + owner // 2, block))
                rhs = jnp.concatenate([tall[o, b] for o, b in where], axis=1)
                s = jnp.dot(lhs, rhs, preferred_element_type=jnp.float32)
                for u in range(2):
                    o, b = where[u]
                    wrow = jnp.broadcast_to(wt[o, b][None], (LANES // 8, 8, LANES)).reshape(LANES, LANES)
                    row = 2 * pair + u
                    carry = jnp.zeros((8, LANES), jnp.float32)
                    for m in range(2):
                        weight = qwb[2 * zq + tile, pl.ds(first + m * LANES, LANES), :]
                        x = s[m * LANES : (m + 1) * LANES, u * LANES : (u + 1) * LANES] * weight * wrow
                        lower, upper = diagonals(x)
                        psum[zq, tile, 2 * part + m, row : row + 1, :] += row_sum(carry + lower)
                        carry = upper
                    psum[zq, tile, 2 * part + 2, row : row + 1, :] += row_sum(carry)
            return 0

        lax.fori_loop(0, NZ, query, 0)
        return 0

    lax.fori_loop(0, CHUNKS, chunk, 0)

    start_p(2)
    prec[z] = psum[z]

    def sent(j, _):
        for g in range(4):
            t_copy(g, j).wait_send()
        for c in range(CHUNKS):
            q_copy(c, j).wait_send()
        return 0

    lax.fori_loop(0, PEERS, sent, 0)
    for k in range(2):
        s2[k].wait_send()
        s1_even[k].wait_send()

    def wait_p(j, _):
        for part in range(3):
            p_copy(part, j).wait()
        return 0

    lax.fori_loop(0, PEERS, wait_p, 0)
    total = prec[0]
    for k in range(1, NZ):
        total = total + prec[k]
    for tile in range(2):
        b = scores([total[tile, m] for m in range(5)])
        mean = jnp.sum(jnp.maximum(b, 0.0), axis=1, keepdims=True) / (5 * LANES)
        line = jnp.sum(jnp.where(position == place, jnp.broadcast_to(mean, (8, LANES)), 0.0), axis=0, keepdims=True)
        resc_ref[tile : tile + 1, :] = line[:, 0:8]


def shards(queries, query_scale, query_mask, query_len, targets, target_scale, target_mask, target_len, hit_ids):
    tiles, rows, width = queries.shape
    blocks, cols, _ = targets.shape
    hits = hit_ids.shape[1]
    depth = width // NZ
    half = rows // 2
    vmem = pltpu.VMEM
    one = (pl.ANY, vmem, vmem, pltpu.SMEM)
    spaces = one + one + (vmem,)
    dma = pltpu.SemaphoreType.DMA
    bf, f32 = jnp.bfloat16, jnp.float32
    band, resc = pl.pallas_call(
        kernel,
        out_shape=(
            jax.ShapeDtypeStruct((2, blocks, tiles, rows + cols), f32),
            jax.ShapeDtypeStruct((tiles, hits), f32),
        ),
        in_specs=[pl.BlockSpec(memory_space=m) for m in spaces],
        out_specs=(pl.BlockSpec(memory_space=pltpu.VMEM),) * 2,
        scratch_shapes=[
            vmem((tiles, rows, width), bf),
            vmem((blocks, cols, width), bf),
            vmem((NZ, blocks, depth, cols), bf),
            vmem((2 * NZ, blocks, depth, cols), bf),
            vmem((NZ, CHUNKS, depth, half), bf),
            vmem((NZ, CHUNKS, depth, half), bf),
            vmem((2, tiles, rows, width), bf),
            vmem((16, LANES), bf),
            vmem((2 * NZ, 16, LANES), bf),
            vmem((2, 16, LANES), bf),
            vmem((2 * NZ, blocks, 8, cols), f32),
            vmem((8, LANES), jnp.int32),
            vmem((NZ, 8, LANES), jnp.int32),
            pltpu.SMEM((NZ, 8, LANES), jnp.int32),
            vmem((NZ * tiles, rows, LANES), f32),
            vmem((2 * tiles, rows, LANES), f32),
            vmem((rows, 2 * LANES), f32),
            vmem((NZ, tiles, 5, hits, LANES), f32),
            vmem((NZ, tiles, 5, hits, LANES), f32),
            vmem((5, 2 * blocks * tiles, LANES), f32),
            vmem((rows, width), bf),
            dma((10,)),
            dma((6,)),
            dma((4, PEERS)), dma((4, PEERS)),
            dma((CHUNKS, PEERS)), dma((CHUNKS, PEERS)),
            dma((4, NZ)), dma((4, NZ)),
            dma((2,)), dma((2,)),
            dma((2,)), dma((2,)),
            dma((2, PEERS)), dma((2, PEERS)),
            dma((3,)), dma((3,)),
            dma((3, PEERS)), dma((3, PEERS)),
            dma((1,)), dma((1,)),
        ],
        compiler_params=pltpu.CompilerParams(
            collective_id=0, has_side_effects=True, vmem_limit_bytes=56 * 1024 * 1024
        ),
    )(queries, query_scale, query_mask, query_len, targets, target_scale, target_mask, target_len, hit_ids)
    return band, resc


def solution(mesh):
    in_specs = (
        P(("db", "pb"), None, None),
        P(("db", "pb"), None),
        P(("db", "pb"), None),
        P(("db", "pb")),
        P(("db", "pb"), None, None),
        P(("db", "pb"), None),
        P(("db", "pb"), None),
        P(("db", "pb")),
        P(("db", "pb"), None),
    )
    out_specs = (P(None, ("db", "pb"), None, None), P(("db", "pb"), None))
    return jax.shard_map(shards, mesh=mesh, in_specs=in_specs, out_specs=out_specs, check_vma=False)
```

```python
import jax
import jax.numpy as jnp
from jax import lax
from jax.experimental import pallas as pl
from jax.experimental.pallas import tpu as pltpu
from jax.sharding import PartitionSpec as P

MESH = pl.DeviceIdType.MESH
LANES = 128
NZ = 8
PEERS = NZ - 1
AHEAD = 4
GROUPS = 2
EACH = 8 // GROUPS
CHUNKS = 4


def kernel(
    q_hbm, qsc, qmk, qln, t_hbm, tsc, tmk, tln, h_in, band_ref, resc_ref,
    qin, tin, ts, tall, qs, qr, qb, wown, wp, wps, wt, hown, hv, hs, qwb, qwbb, sbuf, psum, prec, bo, via,
    in_sem, own_sem, t_send, t_recv, q_send, q_recv, y_send, y_recv, s2_send, s2_recv, s1_send, s1_recv,
    w_send, w_recv, m_send, m_recv, p_send, p_recv, v_send, v_recv,
):
    n_db = lax.axis_size("db")
    db = lax.axis_index("db")
    pb = lax.axis_index("pb")
    z = pb // 2
    yh = lax.rem(pb, 2)
    core = lax.rem(db, 2)
    mate = db + 1 - 2 * core
    last_x = lax.rem(db, 8) >= 6
    first_x = lax.rem(db, 8) < 2
    depth = ts.shape[2]
    half = qs.shape[3]

    def zdev(k):
        return (db, k * 2 + yh)

    def step_of(j):
        far = NZ // 2 - (j + 1) // 2
        return jnp.where(lax.rem(j, 2) == 0, far, NZ - far)

    def to(j):
        return lax.rem(z + step_of(j), NZ)

    def frm(j):
        return lax.rem(z - step_of(j) + NZ, NZ)

    y_dev = (db, pb + 1 - 2 * yh)
    core_dev = (mate, pb)

    def shifted(by):
        return (lax.rem(db + by + n_db, n_db), pb)

    def remote(src, dst, send, recv, dev):
        return pltpu.make_async_remote_copy(
            src_ref=src, dst_ref=dst, send_sem=send, recv_sem=recv, device_id=dev, device_id_type=MESH
        )

    t_loads = [pltpu.make_async_copy(t_hbm.at[b], tin.at[b], in_sem.at[b]) for b in range(8)]
    q_loads = [pltpu.make_async_copy(q_hbm.at[k], qin.at[k], in_sem.at[8 + k]) for k in range(2)]
    for copy in t_loads + q_loads:
        copy.start()

    barrier = pltpu.get_barrier_semaphore()

    def greet(j, _):
        pl.semaphore_signal(barrier, inc=1, device_id=zdev(frm(j)), device_id_type=MESH)
        return 0

    lax.fori_loop(0, PEERS, greet, 0)
    for dev in (y_dev, core_dev, shifted(-1), shifted(-2)):
        pl.semaphore_signal(barrier, inc=1, device_id=dev, device_id_type=MESH)

    @pl.when(last_x)
    def _():
        pl.semaphore_signal(barrier, inc=1, device_id=shifted(8), device_id_type=MESH)

    @pl.when(first_x)
    def _():
        pl.semaphore_signal(barrier, inc=1, device_id=shifted(-10), device_id_type=MESH)

    flip = (
        lax.broadcasted_iota(jnp.int32, (LANES, LANES), 0) + lax.broadcasted_iota(jnp.int32, (LANES, LANES), 1)
        == LANES - 1
    ).astype(jnp.float32).astype(jnp.bfloat16)
    def turn_targets(g):
        for b in range(EACH):
            turned = jnp.dot(tin[EACH * g + b].T, flip, preferred_element_type=jnp.float32).astype(jnp.bfloat16)
            ts[:, EACH * g + b] = turned.reshape(NZ, depth, LANES)

    def t_copy(g, j):
        k = to(j)
        return remote(
            ts.at[k, pl.ds(EACH * g, EACH)], tall.at[z, pl.ds(EACH * g, EACH)], t_send.at[g, j], t_recv.at[g, j], zdev(k)
        )

    def start_targets(g):
        def go(j, _):
            t_copy(g, j).start()
            return 0

        lax.fori_loop(0, PEERS, go, 0)

    for copy in t_loads[:EACH]:
        copy.wait()
    turn_targets(0)
    pl.semaphore_wait(barrier, PEERS + 4 + jnp.where(last_x, 2, 0))

    start_targets(0)

    position = lax.broadcasted_iota(jnp.int32, (8, LANES), 1)
    place = lax.broadcasted_iota(jnp.int32, (8, LANES), 0)
    lengths = jnp.zeros((8, LANES), jnp.int32)
    for b in range(8):
        lengths = jnp.where(place == b, tln[b], lengths)
    t_scale = tsc[...].astype(jnp.float32)
    t_weight = jnp.where(tmk[...] == 1, jnp.where(position < lengths, t_scale, 0.0), 0.0)
    t_weight = jnp.dot(t_weight.astype(jnp.bfloat16), flip, preferred_element_type=jnp.float32)
    q_scale = qsc[...].astype(jnp.float32)
    q_mask = qmk[...]
    q_rows = []
    for k in range(2):
        for m in range(4):
            cols = slice(m * LANES, (m + 1) * LANES)
            at = lax.broadcasted_iota(jnp.int32, (1, LANES), 1) + m * LANES
            kept = jnp.where(at < qln[k], q_scale[k : k + 1, cols], 0.0)
            q_rows.append(jnp.where(q_mask[k : k + 1, cols] == 1, kept, 0.0))
    wown[...] = jnp.concatenate([t_weight] + q_rows, axis=0).astype(jnp.bfloat16)
    hown[...] = jnp.concatenate([h_in[0:1], h_in[1:2], jnp.zeros((1, LANES - 16), jnp.int32)], axis=1)

    shift_w = [remote(wown, wps.at[i], m_send.at[i], m_recv.at[i], shifted(i + 1)) for i in range(2)]
    for copy in shift_w:
        copy.start()

    def small(j):
        dev = zdev(to(j))
        return [
            remote(wown, wp.at[z], w_send.at[0, j], w_recv.at[0, j], dev),
            remote(hown, hv.at[z], w_send.at[1, j], w_recv.at[1, j], dev),
        ]

    def start_small(j, _):
        for copy in small(j):
            copy.start()
        return 0

    lax.fori_loop(0, PEERS, start_small, 0)
    own_small = [
        pltpu.make_async_copy(wown, wp.at[z], own_sem.at[0]),
        pltpu.make_async_copy(hown, hv.at[z], own_sem.at[1]),
    ]
    for copy in own_small:
        copy.start()

    s2 = [remote(q_hbm.at[k], qb.at[1, k], s2_send.at[k], s2_recv.at[k], shifted(2)) for k in range(2)]
    s1_even = [remote(q_hbm.at[k], qb.at[0, k], s1_send.at[k], s1_recv.at[k], core_dev) for k in range(2)]
    s1_odd = [remote(qb.at[1, k], qb.at[0, k], s1_send.at[k], s1_recv.at[k], core_dev) for k in range(2)]
    s2_first = remote(q_hbm.at[1], via, v_send.at[0], v_recv.at[0], shifted(8))
    s2_then = remote(via, qb.at[1, 1], s2_send.at[1], s2_recv.at[1], shifted(10))
    s2[0].start()

    @pl.when(last_x)
    def _():
        s2_first.start()

    @pl.when(jnp.logical_not(last_x))
    def _():
        s2[1].start()

    @pl.when(core == 0)
    def _():
        for copy in s1_even:
            copy.start()

    for copy in t_loads[EACH:]:
        copy.wait()

    def send_targets(g, _):
        turn_targets(g)

        @pl.when(g < AHEAD)
        def _():
            start_targets(g)

        return 0

    lax.fori_loop(1, GROUPS, send_targets, 0)
    own_t = pltpu.make_async_copy(ts.at[z], tall.at[z], own_sem.at[3])
    own_t.start()

    for copy in q_loads:
        copy.wait()

    def q_copy(c, j):
        k = to(j)
        return remote(qs.at[k, c], qr.at[z, c], q_send.at[c, j], q_recv.at[c, j], zdev(k))

    def start_chunk(c):
        def go(j, _):
            q_copy(c, j).start()
            return 0

        lax.fori_loop(0, PEERS, go, 0)

    def turn_queries(c, _):
        rows = pl.ds(pl.multiple_of(lax.rem(c, 2) * half, half), half)
        turned = qin[c // 2, rows, :].T
        qs[:, c] = turned.reshape(NZ, depth, half)

        @pl.when(c + GROUPS < AHEAD)
        def _():
            start_chunk(c)

        return 0

    lax.fori_loop(0, CHUNKS, turn_queries, 0)
    own_q = pltpu.make_async_copy(qs.at[z], qr.at[z], own_sem.at[4])
    own_q.start()

    def y_copy(g, i, src):
        part = pl.ds(EACH * g, EACH)
        return remote(tall.at[src, part], tall.at[NZ + src, part], y_send.at[g, i], y_recv.at[g, i], y_dev)

    own_t.wait()

    def pass_on(g, _):
        y_copy(g, PEERS, z).start()

        def go(j, _):
            t_copy(g, j).wait_recv()
            y_copy(g, j, frm(j)).start()
            later = g + AHEAD

            @pl.when(later < GROUPS)
            def _():
                t_copy(later, j).start()

            @pl.when(jnp.logical_and(later >= GROUPS, later < GROUPS + CHUNKS))
            def _():
                q_copy(later - GROUPS, j).start()

            return 0

        lax.fori_loop(0, PEERS, go, 0)

        @pl.when(jnp.logical_and(g == 0, last_x))
        def _():
            s2_first.wait()
            s2_then.start()

        return 0

    lax.fori_loop(0, GROUPS, pass_on, 0)

    def wait_small(j, _):
        for copy in small(j):
            copy.wait()
        return 0

    lax.fori_loop(0, PEERS, wait_small, 0)
    for copy in own_small:
        copy.wait()
    to_scalars = pltpu.make_async_copy(hv, hs, own_sem.at[5])
    to_scalars.start()
    for copy in shift_w:
        copy.wait()
    y_small = remote(wp.at[pl.ds(0, NZ)], wp.at[pl.ds(NZ, NZ)], m_send.at[2], m_recv.at[2], y_dev)
    y_small.start()

    def spread(row):
        return jnp.broadcast_to(row, (LANES, LANES)).T

    def spread_all(i, _):
        w = wp[i].astype(jnp.float32)
        for m in range(8):
            rows = pl.ds((m % 4) * LANES, LANES)
            qwb[2 * i + m // 4, rows, :] = spread(w[8 + m : 9 + m])
        return 0

    lax.fori_loop(0, NZ, spread_all, 0)

    def widen(o, _):
        w = wp[o].astype(jnp.float32)
        for b in range(8):
            wt[o, b] = jnp.broadcast_to(w[b : b + 1], (8, LANES))
        return 0

    lax.fori_loop(0, NZ, widen, 0)

    def spread_shift(i, _):
        w = wps[i].astype(jnp.float32)
        for m in range(8):
            rows = pl.ds((m % 4) * LANES, LANES)
            qwbb[2 * i + m // 4, rows, :] = spread(w[8 + m : 9 + m])
        return 0

    lax.fori_loop(0, 2, spread_shift, 0)

    def chunk_arrived(c):
        def go(j, _):
            q_copy(c, j).wait_recv()
            later = c + AHEAD

            @pl.when(later < CHUNKS)
            def _():
                q_copy(later, j).start()

            return 0

        lax.fori_loop(0, PEERS, go, 0)

    chunk_arrived(0)

    low = lax.broadcasted_iota(jnp.int32, (LANES, LANES), 1) >= lax.broadcasted_iota(jnp.int32, (LANES, LANES), 0)

    def diagonals(x):
        y = pltpu.roll(x, 0, 1, stride=1, stride_axis=0)
        lower = jnp.where(low, y, 0.0).reshape(LANES // 8, 8, LANES)
        upper = jnp.where(low, 0.0, y).reshape(LANES // 8, 8, LANES)
        return jnp.sum(lower, axis=0), jnp.sum(upper, axis=0)

    def row_sum(v):
        return jnp.sum(v, axis=0, keepdims=True)

    for k in range(2):
        s2[k].wait_recv()

    @pl.when(core == 1)
    def _():
        for copy in s1_odd:
            copy.start()

    def bands(s, k):
        def pair(p, _):
            rhs = jnp.concatenate(
                [ts[:, 2 * p].reshape(NZ * depth, LANES), ts[:, 2 * p + 1].reshape(NZ * depth, LANES)], axis=1
            )
            sbuf[...] = jnp.dot(qb[s, k], rhs, preferred_element_type=jnp.float32)
            for u in range(2):
                w8 = wt[z, 2 * p + u]
                wrow = jnp.broadcast_to(w8[None], (LANES // 8, 8, LANES)).reshape(LANES, LANES)
                row = (s * 8 + 2 * p + u) * 2 + k
                carry = jnp.zeros((8, LANES), jnp.float32)
                for m in range(4):
                    rows = pl.ds(m * LANES, LANES)
                    x = sbuf[rows, u * LANES : (u + 1) * LANES] * qwbb[2 * s + k, rows, :] * wrow
                    lower, upper = diagonals(x)
                    bo[m, pl.ds(row, 1), :] = row_sum(carry + lower)
                    carry = upper
                bo[4, pl.ds(row, 1), :] = row_sum(carry)
            return 0

        lax.fori_loop(0, 4, pair, 0)

    lax.fori_loop(0, 2, lambda k, c: (bands(1, k), c)[1], 0)
    chunk_arrived(1)
    for k in range(2):
        s1_even[k].wait_recv()
    lax.fori_loop(0, 2, lambda k, c: (bands(0, k), c)[1], 0)

    def scores(segments):
        g = jnp.concatenate(segments, axis=1)
        return g + pltpu.roll(g, 1, 1)

    band = scores([bo[m] for m in range(5)])
    for s in range(2):
        for t in range(8):
            band_ref[s, t] = band[(s * 8 + t) * 2 : (s * 8 + t) * 2 + 2]

    own_q.wait()
    to_scalars.wait()
    y_small.wait()
    lax.fori_loop(NZ, 2 * NZ, widen, 0)
    psum[...] = jnp.zeros_like(psum)

    def wait_y(g, _):
        def go(j, _):
            y_copy(g, j, frm(j)).wait()
            return 0

        lax.fori_loop(0, PEERS, go, 0)
        y_copy(g, PEERS, z).wait()
        return 0

    lax.fori_loop(0, GROUPS, wait_y, 0)

    def p_copy(part, j):
        k = to(j)
        tile, seg, count = ((0, 0, 5), (1, 0, 2), (1, 2, 3))[part]
        return remote(
            psum.at[k, tile, pl.ds(seg, count)], prec.at[z, tile, pl.ds(seg, count)],
            p_send.at[part, j], p_recv.at[part, j], zdev(k),
        )

    def start_p(part):
        def go(j, _):
            p_copy(part, j).start()
            return 0

        lax.fori_loop(0, PEERS, go, 0)

    def chunk(c, _):
        @pl.when(c >= 2)
        def _():
            chunk_arrived(c)

        @pl.when(c == CHUNKS - 1)
        def _():
            start_p(0)
            start_p(1)

        tile, part = c // 2, lax.rem(c, 2)
        first = pl.multiple_of(part * half, half)

        def query(zq, _):
            lhs = qr[zq, c].T
            for pair in range(4):
                where = []
                for u in range(2):
                    hit = lax.rem(hs[zq, 0, tile * 8 + 2 * pair + u], 2 * NZ * 8)
                    owner, block = hit // 8, lax.rem(hit, 8)
                    other = jnp.where(lax.rem(owner, 2) == yh, 0, NZ)
                    where.append((other + owner // 2, block))
                rhs = jnp.concatenate([tall[o, b] for o, b in where], axis=1)
                s = jnp.dot(lhs, rhs, preferred_element_type=jnp.float32)
                for u in range(2):
                    o, b = where[u]
                    wrow = jnp.broadcast_to(wt[o, b][None], (LANES // 8, 8, LANES)).reshape(LANES, LANES)
                    row = 2 * pair + u
                    carry = jnp.zeros((8, LANES), jnp.float32)
                    for m in range(2):
                        weight = qwb[2 * zq + tile, pl.ds(first + m * LANES, LANES), :]
                        x = s[m * LANES : (m + 1) * LANES, u * LANES : (u + 1) * LANES] * weight * wrow
                        lower, upper = diagonals(x)
                        psum[zq, tile, 2 * part + m, row : row + 1, :] += row_sum(carry + lower)
                        carry = upper
                    psum[zq, tile, 2 * part + 2, row : row + 1, :] += row_sum(carry)
            return 0

        lax.fori_loop(0, NZ, query, 0)
        return 0

    lax.fori_loop(0, CHUNKS, chunk, 0)

    start_p(2)
    prec[z] = psum[z]

    def sent(j, _):
        for g in range(GROUPS):
            t_copy(g, j).wait_send()
        for c in range(CHUNKS):
            q_copy(c, j).wait_send()
        return 0

    lax.fori_loop(0, PEERS, sent, 0)
    for k in range(2):
        s2[k].wait_send()
        s1_even[k].wait_send()

    def wait_p(j, _):
        for part in range(3):
            p_copy(part, j).wait()
        return 0

    lax.fori_loop(0, PEERS, wait_p, 0)
    total = prec[0]
    for k in range(1, NZ):
        total = total + prec[k]
    for tile in range(2):
        b = scores([total[tile, m] for m in range(5)])
        mean = jnp.sum(jnp.maximum(b, 0.0), axis=1, keepdims=True) / (5 * LANES)
        line = jnp.sum(jnp.where(position == place, jnp.broadcast_to(mean, (8, LANES)), 0.0), axis=0, keepdims=True)
        resc_ref[tile : tile + 1, :] = line[:, 0:8]


def shards(queries, query_scale, query_mask, query_len, targets, target_scale, target_mask, target_len, hit_ids):
    tiles, rows, width = queries.shape
    blocks, cols, _ = targets.shape
    hits = hit_ids.shape[1]
    depth = width // NZ
    half = rows // 2
    vmem = pltpu.VMEM
    one = (pl.ANY, vmem, vmem, pltpu.SMEM)
    spaces = one + one + (vmem,)
    dma = pltpu.SemaphoreType.DMA
    bf, f32 = jnp.bfloat16, jnp.float32
    band, resc = pl.pallas_call(
        kernel,
        out_shape=(
            jax.ShapeDtypeStruct((2, blocks, tiles, rows + cols), f32),
            jax.ShapeDtypeStruct((tiles, hits), f32),
        ),
        in_specs=[pl.BlockSpec(memory_space=m) for m in spaces],
        out_specs=(pl.BlockSpec(memory_space=pltpu.VMEM),) * 2,
        scratch_shapes=[
            vmem((tiles, rows, width), bf),
            vmem((blocks, cols, width), bf),
            vmem((NZ, blocks, depth, cols), bf),
            vmem((2 * NZ, blocks, depth, cols), bf),
            vmem((NZ, CHUNKS, depth, half), bf),
            vmem((NZ, CHUNKS, depth, half), bf),
            vmem((2, tiles, rows, width), bf),
            vmem((16, LANES), bf),
            vmem((2 * NZ, 16, LANES), bf),
            vmem((2, 16, LANES), bf),
            vmem((2 * NZ, blocks, 8, cols), f32),
            vmem((1, LANES), jnp.int32),
            vmem((NZ, 1, LANES), jnp.int32),
            pltpu.SMEM((NZ, 1, LANES), jnp.int32),
            vmem((NZ * tiles, rows, LANES), f32),
            vmem((2 * tiles, rows, LANES), f32),
            vmem((rows, 2 * LANES), f32),
            vmem((NZ, tiles, 5, hits, LANES), f32),
            vmem((NZ, tiles, 5, hits, LANES), f32),
            vmem((5, 2 * blocks * tiles, LANES), f32),
            vmem((rows, width), bf),
            dma((10,)),
            dma((6,)),
            dma((GROUPS, PEERS)), dma((GROUPS, PEERS)),
            dma((CHUNKS, PEERS)), dma((CHUNKS, PEERS)),
            dma((GROUPS, NZ)), dma((GROUPS, NZ)),
            dma((2,)), dma((2,)),
            dma((2,)), dma((2,)),
            dma((2, PEERS)), dma((2, PEERS)),
            dma((3,)), dma((3,)),
            dma((3, PEERS)), dma((3, PEERS)),
            dma((1,)), dma((1,)),
        ],
        compiler_params=pltpu.CompilerParams(
            collective_id=0, has_side_effects=True, vmem_limit_bytes=56 * 1024 * 1024
        ),
    )(queries, query_scale, query_mask, query_len, targets, target_scale, target_mask, target_len, hit_ids)
    return band, resc


def solution(mesh):
    in_specs = (
        P(("db", "pb"), None, None),
        P(("db", "pb"), None),
        P(("db", "pb"), None),
        P(("db", "pb")),
        P(("db", "pb"), None, None),
        P(("db", "pb"), None),
        P(("db", "pb"), None),
        P(("db", "pb")),
        P(("db", "pb"), None),
    )
    out_specs = (P(None, ("db", "pb"), None, None), P(("db", "pb"), None))
    return jax.shard_map(shards, mesh=mesh, in_specs=in_specs, out_specs=out_specs, check_vma=False)
```

```python
import jax
import jax.numpy as jnp
from jax import lax
from jax.experimental import pallas as pl
from jax.experimental.pallas import tpu as pltpu
from jax.sharding import PartitionSpec as P

MESH = pl.DeviceIdType.MESH
LANES = 128
NZ = 8
PEERS = NZ - 1
AHEAD = 5
GROUPS = 2
EACH = 8 // GROUPS
CHUNKS = 4


def kernel(
    q_hbm, qsc, qmk, qln, t_hbm, tsc, tmk, tln, h_in, band_ref, resc_ref,
    qin, tin, ts, tall, qs, qr, qb, wown, wp, wps, wt, hown, hv, hs, qwb, qwbb, sbuf, psum, prec, bo, via,
    in_sem, own_sem, t_send, t_recv, q_send, q_recv, y_send, y_recv, s2_send, s2_recv, s1_send, s1_recv,
    w_send, w_recv, m_send, m_recv, p_send, p_recv, v_send, v_recv,
):
    n_db = lax.axis_size("db")
    db = lax.axis_index("db")
    pb = lax.axis_index("pb")
    z = pb // 2
    yh = lax.rem(pb, 2)
    core = lax.rem(db, 2)
    mate = db + 1 - 2 * core
    last_x = lax.rem(db, 8) >= 6
    first_x = lax.rem(db, 8) < 2
    depth = ts.shape[2]
    half = qs.shape[3]

    def zdev(k):
        return (db, k * 2 + yh)

    def step_of(j):
        far = NZ // 2 - (j + 1) // 2
        return jnp.where(lax.rem(j, 2) == 0, far, NZ - far)

    def to(j):
        return lax.rem(z + step_of(j), NZ)

    def frm(j):
        return lax.rem(z - step_of(j) + NZ, NZ)

    y_dev = (db, pb + 1 - 2 * yh)
    core_dev = (mate, pb)

    def shifted(by):
        return (lax.rem(db + by + n_db, n_db), pb)

    def remote(src, dst, send, recv, dev):
        return pltpu.make_async_remote_copy(
            src_ref=src, dst_ref=dst, send_sem=send, recv_sem=recv, device_id=dev, device_id_type=MESH
        )

    t_loads = [pltpu.make_async_copy(t_hbm.at[b], tin.at[b], in_sem.at[b]) for b in range(8)]
    q_loads = [pltpu.make_async_copy(q_hbm.at[k], qin.at[k], in_sem.at[8 + k]) for k in range(2)]
    for copy in t_loads[:EACH]:
        copy.start()

    barrier = pltpu.get_barrier_semaphore()

    def greet(j, _):
        pl.semaphore_signal(barrier, inc=1, device_id=zdev(frm(j)), device_id_type=MESH)
        return 0

    lax.fori_loop(0, PEERS, greet, 0)
    for dev in (y_dev, core_dev, shifted(-1), shifted(-2)):
        pl.semaphore_signal(barrier, inc=1, device_id=dev, device_id_type=MESH)

    @pl.when(last_x)
    def _():
        pl.semaphore_signal(barrier, inc=1, device_id=shifted(8), device_id_type=MESH)

    @pl.when(first_x)
    def _():
        pl.semaphore_signal(barrier, inc=1, device_id=shifted(-10), device_id_type=MESH)

    flip = (
        lax.broadcasted_iota(jnp.int32, (LANES, LANES), 0) + lax.broadcasted_iota(jnp.int32, (LANES, LANES), 1)
        == LANES - 1
    ).astype(jnp.float32).astype(jnp.bfloat16)
    def turn_targets(g):
        for b in range(EACH):
            turned = jnp.dot(tin[EACH * g + b].T, flip, preferred_element_type=jnp.float32).astype(jnp.bfloat16)
            ts[:, EACH * g + b] = turned.reshape(NZ, depth, LANES)

    def t_copy(g, j):
        k = to(j)
        return remote(
            ts.at[k, pl.ds(EACH * g, EACH)], tall.at[z, pl.ds(EACH * g, EACH)], t_send.at[g, j], t_recv.at[g, j], zdev(k)
        )

    def start_targets(g):
        def go(j, _):
            t_copy(g, j).start()
            return 0

        lax.fori_loop(0, PEERS, go, 0)

    for copy in t_loads[:EACH]:
        copy.wait()
    for copy in t_loads[EACH:] + q_loads:
        copy.start()
    turn_targets(0)
    pl.semaphore_wait(barrier, PEERS + 4 + jnp.where(last_x, 2, 0))

    start_targets(0)

    position = lax.broadcasted_iota(jnp.int32, (8, LANES), 1)
    place = lax.broadcasted_iota(jnp.int32, (8, LANES), 0)
    lengths = jnp.zeros((8, LANES), jnp.int32)
    for b in range(8):
        lengths = jnp.where(place == b, tln[b], lengths)
    t_scale = tsc[...].astype(jnp.float32)
    t_weight = jnp.where(tmk[...] == 1, jnp.where(position < lengths, t_scale, 0.0), 0.0)
    t_weight = jnp.dot(t_weight.astype(jnp.bfloat16), flip, preferred_element_type=jnp.float32)
    q_scale = qsc[...].astype(jnp.float32)
    q_mask = qmk[...]
    q_rows = []
    for k in range(2):
        for m in range(4):
            cols = slice(m * LANES, (m + 1) * LANES)
            at = lax.broadcasted_iota(jnp.int32, (1, LANES), 1) + m * LANES
            kept = jnp.where(at < qln[k], q_scale[k : k + 1, cols], 0.0)
            q_rows.append(jnp.where(q_mask[k : k + 1, cols] == 1, kept, 0.0))
    wown[...] = jnp.concatenate([t_weight] + q_rows, axis=0).astype(jnp.bfloat16)
    hown[...] = jnp.concatenate([h_in[0:1], h_in[1:2], jnp.zeros((1, LANES - 16), jnp.int32)], axis=1)

    shift_w = [remote(wown, wps.at[i], m_send.at[i], m_recv.at[i], shifted(i + 1)) for i in range(2)]
    for copy in shift_w:
        copy.start()

    def small(j):
        dev = zdev(to(j))
        return [
            remote(wown, wp.at[z], w_send.at[0, j], w_recv.at[0, j], dev),
            remote(hown, hv.at[z], w_send.at[1, j], w_recv.at[1, j], dev),
        ]

    def start_small(j, _):
        for copy in small(j):
            copy.start()
        return 0

    lax.fori_loop(0, PEERS, start_small, 0)
    own_small = [
        pltpu.make_async_copy(wown, wp.at[z], own_sem.at[0]),
        pltpu.make_async_copy(hown, hv.at[z], own_sem.at[1]),
    ]
    for copy in own_small:
        copy.start()

    s2 = [remote(q_hbm.at[k], qb.at[1, k], s2_send.at[k], s2_recv.at[k], shifted(2)) for k in range(2)]
    s1_even = [remote(q_hbm.at[k], qb.at[0, k], s1_send.at[k], s1_recv.at[k], core_dev) for k in range(2)]
    s1_odd = [remote(qb.at[1, k], qb.at[0, k], s1_send.at[k], s1_recv.at[k], core_dev) for k in range(2)]
    s2_first = remote(q_hbm.at[1], via, v_send.at[0], v_recv.at[0], shifted(8))
    s2_then = remote(via, qb.at[1, 1], s2_send.at[1], s2_recv.at[1], shifted(10))
    s2[0].start()

    @pl.when(last_x)
    def _():
        s2_first.start()

    @pl.when(jnp.logical_not(last_x))
    def _():
        s2[1].start()

    @pl.when(core == 0)
    def _():
        for copy in s1_even:
            copy.start()

    for copy in t_loads[EACH:]:
        copy.wait()

    def send_targets(g, _):
        turn_targets(g)

        @pl.when(g < AHEAD)
        def _():
            start_targets(g)

        return 0

    lax.fori_loop(1, GROUPS, send_targets, 0)
    own_t = pltpu.make_async_copy(ts.at[z], tall.at[z], own_sem.at[3])
    own_t.start()

    for copy in q_loads:
        copy.wait()

    def q_copy(c, j):
        k = to(j)
        return remote(qs.at[k, c], qr.at[z, c], q_send.at[c, j], q_recv.at[c, j], zdev(k))

    def start_chunk(c):
        def go(j, _):
            q_copy(c, j).start()
            return 0

        lax.fori_loop(0, PEERS, go, 0)

    def turn_queries(c, _):
        rows = pl.ds(pl.multiple_of(lax.rem(c, 2) * half, half), half)
        turned = qin[c // 2, rows, :].T
        qs[:, c] = turned.reshape(NZ, depth, half)

        @pl.when(c + GROUPS < AHEAD)
        def _():
            start_chunk(c)

        return 0

    lax.fori_loop(0, CHUNKS, turn_queries, 0)
    own_q = pltpu.make_async_copy(qs.at[z], qr.at[z], own_sem.at[4])
    own_q.start()

    def y_copy(g, i, src):
        part = pl.ds(EACH * g, EACH)
        return remote(tall.at[src, part], tall.at[NZ + src, part], y_send.at[g, i], y_recv.at[g, i], y_dev)

    own_t.wait()

    def pass_on(g, _):
        y_copy(g, PEERS, z).start()

        def go(j, _):
            t_copy(g, j).wait_recv()
            y_copy(g, j, frm(j)).start()
            later = g + AHEAD

            @pl.when(later < GROUPS)
            def _():
                t_copy(later, j).start()

            @pl.when(jnp.logical_and(later >= GROUPS, later < GROUPS + CHUNKS))
            def _():
                q_copy(later - GROUPS, j).start()

            return 0

        lax.fori_loop(0, PEERS, go, 0)

        @pl.when(jnp.logical_and(g == 0, last_x))
        def _():
            s2_first.wait()
            s2_then.start()

        return 0

    lax.fori_loop(0, GROUPS, pass_on, 0)

    def wait_small(j, _):
        for copy in small(j):
            copy.wait()
        return 0

    lax.fori_loop(0, PEERS, wait_small, 0)
    for copy in own_small:
        copy.wait()
    to_scalars = pltpu.make_async_copy(hv, hs, own_sem.at[5])
    to_scalars.start()
    for copy in shift_w:
        copy.wait()
    y_small = remote(wp.at[pl.ds(0, NZ)], wp.at[pl.ds(NZ, NZ)], m_send.at[2], m_recv.at[2], y_dev)
    y_small.start()

    def spread(row):
        return jnp.broadcast_to(row, (LANES, LANES)).T

    def spread_all(i, _):
        w = wp[i].astype(jnp.float32)
        for m in range(8):
            rows = pl.ds((m % 4) * LANES, LANES)
            qwb[2 * i + m // 4, rows, :] = spread(w[8 + m : 9 + m])
        return 0

    lax.fori_loop(0, NZ, spread_all, 0)

    def widen(o, _):
        w = wp[o].astype(jnp.float32)
        for b in range(8):
            wt[o, b] = jnp.broadcast_to(w[b : b + 1], (8, LANES))
        return 0

    lax.fori_loop(0, NZ, widen, 0)

    def spread_shift(i, _):
        w = wps[i].astype(jnp.float32)
        for m in range(8):
            rows = pl.ds((m % 4) * LANES, LANES)
            qwbb[2 * i + m // 4, rows, :] = spread(w[8 + m : 9 + m])
        return 0

    lax.fori_loop(0, 2, spread_shift, 0)

    def chunk_arrived(c):
        def go(j, _):
            q_copy(c, j).wait_recv()
            later = c + AHEAD

            @pl.when(later < CHUNKS)
            def _():
                q_copy(later, j).start()

            return 0

        lax.fori_loop(0, PEERS, go, 0)

    chunk_arrived(0)

    low = lax.broadcasted_iota(jnp.int32, (LANES, LANES), 1) >= lax.broadcasted_iota(jnp.int32, (LANES, LANES), 0)

    def diagonals(x):
        y = pltpu.roll(x, 0, 1, stride=1, stride_axis=0)
        lower = jnp.where(low, y, 0.0).reshape(LANES // 8, 8, LANES)
        upper = jnp.where(low, 0.0, y).reshape(LANES // 8, 8, LANES)
        return jnp.sum(lower, axis=0), jnp.sum(upper, axis=0)

    def row_sum(v):
        return jnp.sum(v, axis=0, keepdims=True)

    for k in range(2):
        s2[k].wait_recv()

    @pl.when(core == 1)
    def _():
        for copy in s1_odd:
            copy.start()

    def bands(s, k):
        def pair(p, _):
            rhs = jnp.concatenate(
                [ts[:, 2 * p].reshape(NZ * depth, LANES), ts[:, 2 * p + 1].reshape(NZ * depth, LANES)], axis=1
            )
            sbuf[...] = jnp.dot(qb[s, k], rhs, preferred_element_type=jnp.float32)
            for u in range(2):
                w8 = wt[z, 2 * p + u]
                wrow = jnp.broadcast_to(w8[None], (LANES // 8, 8, LANES)).reshape(LANES, LANES)
                row = (s * 8 + 2 * p + u) * 2 + k
                carry = jnp.zeros((8, LANES), jnp.float32)
                for m in range(4):
                    rows = pl.ds(m * LANES, LANES)
                    x = sbuf[rows, u * LANES : (u + 1) * LANES] * qwbb[2 * s + k, rows, :] * wrow
                    lower, upper = diagonals(x)
                    bo[m, pl.ds(row, 1), :] = row_sum(carry + lower)
                    carry = upper
                bo[4, pl.ds(row, 1), :] = row_sum(carry)
            return 0

        lax.fori_loop(0, 4, pair, 0)

    lax.fori_loop(0, 2, lambda k, c: (bands(1, k), c)[1], 0)
    chunk_arrived(1)
    for k in range(2):
        s1_even[k].wait_recv()
    lax.fori_loop(0, 2, lambda k, c: (bands(0, k), c)[1], 0)

    def scores(segments):
        g = jnp.concatenate(segments, axis=1)
        return g + pltpu.roll(g, 1, 1)

    band = scores([bo[m] for m in range(5)])
    for s in range(2):
        for t in range(8):
            band_ref[s, t] = band[(s * 8 + t) * 2 : (s * 8 + t) * 2 + 2]

    own_q.wait()
    to_scalars.wait()
    y_small.wait()
    lax.fori_loop(NZ, 2 * NZ, widen, 0)
    psum[...] = jnp.zeros_like(psum)

    def wait_y(g, _):
        def go(j, _):
            y_copy(g, j, frm(j)).wait()
            return 0

        lax.fori_loop(0, PEERS, go, 0)
        y_copy(g, PEERS, z).wait()
        return 0

    lax.fori_loop(0, GROUPS, wait_y, 0)

    def p_copy(part, j):
        k = to(j)
        tile, seg, count = ((0, 0, 5), (1, 0, 2), (1, 2, 3))[part]
        return remote(
            psum.at[k, tile, pl.ds(seg, count)], prec.at[z, tile, pl.ds(seg, count)],
            p_send.at[part, j], p_recv.at[part, j], zdev(k),
        )

    def start_p(part):
        def go(j, _):
            p_copy(part, j).start()
            return 0

        lax.fori_loop(0, PEERS, go, 0)

    def chunk(c, _):
        @pl.when(c >= 2)
        def _():
            chunk_arrived(c)

        @pl.when(c == CHUNKS - 1)
        def _():
            start_p(0)
            start_p(1)

        tile, part = c // 2, lax.rem(c, 2)
        first = pl.multiple_of(part * half, half)

        def query(zq, _):
            lhs = qr[zq, c].T
            for pair in range(4):
                where = []
                for u in range(2):
                    hit = lax.rem(hs[zq, 0, tile * 8 + 2 * pair + u], 2 * NZ * 8)
                    owner, block = hit // 8, lax.rem(hit, 8)
                    other = jnp.where(lax.rem(owner, 2) == yh, 0, NZ)
                    where.append((other + owner // 2, block))
                rhs = jnp.concatenate([tall[o, b] for o, b in where], axis=1)
                s = jnp.dot(lhs, rhs, preferred_element_type=jnp.float32)
                for u in range(2):
                    o, b = where[u]
                    wrow = jnp.broadcast_to(wt[o, b][None], (LANES // 8, 8, LANES)).reshape(LANES, LANES)
                    row = 2 * pair + u
                    carry = jnp.zeros((8, LANES), jnp.float32)
                    for m in range(2):
                        weight = qwb[2 * zq + tile, pl.ds(first + m * LANES, LANES), :]
                        x = s[m * LANES : (m + 1) * LANES, u * LANES : (u + 1) * LANES] * weight * wrow
                        lower, upper = diagonals(x)
                        psum[zq, tile, 2 * part + m, row : row + 1, :] += row_sum(carry + lower)
                        carry = upper
                    psum[zq, tile, 2 * part + 2, row : row + 1, :] += row_sum(carry)
            return 0

        def peer(j, _):
            query(to(j), 0)

            @pl.when(jnp.logical_and(c == CHUNKS - 1, j < PEERS))
            def _():
                p_copy(2, j).start()

            return 0

        lax.fori_loop(0, NZ, peer, 0)
        return 0

    lax.fori_loop(0, CHUNKS, chunk, 0)

    prec[z] = psum[z]

    def sent(j, _):
        for g in range(GROUPS):
            t_copy(g, j).wait_send()
        for c in range(CHUNKS):
            q_copy(c, j).wait_send()
        return 0

    lax.fori_loop(0, PEERS, sent, 0)
    for k in range(2):
        s2[k].wait_send()
        s1_even[k].wait_send()

    def wait_p(j, _):
        for part in range(3):
            p_copy(part, j).wait()
        return 0

    lax.fori_loop(0, PEERS, wait_p, 0)
    total = prec[0]
    for k in range(1, NZ):
        total = total + prec[k]
    for tile in range(2):
        b = scores([total[tile, m] for m in range(5)])
        mean = jnp.sum(jnp.maximum(b, 0.0), axis=1, keepdims=True) / (5 * LANES)
        line = jnp.sum(jnp.where(position == place, jnp.broadcast_to(mean, (8, LANES)), 0.0), axis=0, keepdims=True)
        resc_ref[tile : tile + 1, :] = line[:, 0:8]


def shards(queries, query_scale, query_mask, query_len, targets, target_scale, target_mask, target_len, hit_ids):
    tiles, rows, width = queries.shape
    blocks, cols, _ = targets.shape
    hits = hit_ids.shape[1]
    depth = width // NZ
    half = rows // 2
    vmem = pltpu.VMEM
    one = (pl.ANY, vmem, vmem, pltpu.SMEM)
    spaces = one + one + (vmem,)
    dma = pltpu.SemaphoreType.DMA
    bf, f32 = jnp.bfloat16, jnp.float32
    band, resc = pl.pallas_call(
        kernel,
        out_shape=(
            jax.ShapeDtypeStruct((2, blocks, tiles, rows + cols), f32),
            jax.ShapeDtypeStruct((tiles, hits), f32),
        ),
        in_specs=[pl.BlockSpec(memory_space=m) for m in spaces],
        out_specs=(pl.BlockSpec(memory_space=pltpu.VMEM),) * 2,
        scratch_shapes=[
            vmem((tiles, rows, width), bf),
            vmem((blocks, cols, width), bf),
            vmem((NZ, blocks, depth, cols), bf),
            vmem((2 * NZ, blocks, depth, cols), bf),
            vmem((NZ, CHUNKS, depth, half), bf),
            vmem((NZ, CHUNKS, depth, half), bf),
            vmem((2, tiles, rows, width), bf),
            vmem((16, LANES), bf),
            vmem((2 * NZ, 16, LANES), bf),
            vmem((2, 16, LANES), bf),
            vmem((2 * NZ, blocks, 8, cols), f32),
            vmem((1, LANES), jnp.int32),
            vmem((NZ, 1, LANES), jnp.int32),
            pltpu.SMEM((NZ, 1, LANES), jnp.int32),
            vmem((NZ * tiles, rows, LANES), f32),
            vmem((2 * tiles, rows, LANES), f32),
            vmem((rows, 2 * LANES), f32),
            vmem((NZ, tiles, 5, hits, LANES), f32),
            vmem((NZ, tiles, 5, hits, LANES), f32),
            vmem((5, 2 * blocks * tiles, LANES), f32),
            vmem((rows, width), bf),
            dma((10,)),
            dma((6,)),
            dma((GROUPS, PEERS)), dma((GROUPS, PEERS)),
            dma((CHUNKS, PEERS)), dma((CHUNKS, PEERS)),
            dma((GROUPS, NZ)), dma((GROUPS, NZ)),
            dma((2,)), dma((2,)),
            dma((2,)), dma((2,)),
            dma((2, PEERS)), dma((2, PEERS)),
            dma((3,)), dma((3,)),
            dma((3, PEERS)), dma((3, PEERS)),
            dma((1,)), dma((1,)),
        ],
        compiler_params=pltpu.CompilerParams(
            collective_id=0, has_side_effects=True, vmem_limit_bytes=56 * 1024 * 1024
        ),
    )(queries, query_scale, query_mask, query_len, targets, target_scale, target_mask, target_len, hit_ids)
    return band, resc


def solution(mesh):
    in_specs = (
        P(("db", "pb"), None, None),
        P(("db", "pb"), None),
        P(("db", "pb"), None),
        P(("db", "pb")),
        P(("db", "pb"), None, None),
        P(("db", "pb"), None),
        P(("db", "pb"), None),
        P(("db", "pb")),
        P(("db", "pb"), None),
    )
    out_specs = (P(None, ("db", "pb"), None, None), P(("db", "pb"), None))
    return jax.shard_map(shards, mesh=mesh, in_specs=in_specs, out_specs=out_specs, check_vma=False)
```

```python
import jax
import jax.numpy as jnp
from jax import lax
from jax.experimental import pallas as pl
from jax.experimental.pallas import tpu as pltpu
from jax.sharding import PartitionSpec as P

MESH = pl.DeviceIdType.MESH
LANES = 128
NZ = 8
PEERS = NZ - 1
AHEAD = 4
GROUPS = 2
EACH = 8 // GROUPS
CHUNKS = 4


def kernel(
    q_hbm, qsc, qmk, qln, t_hbm, tsc, tmk, tln, h_in, band_ref, resc_ref,
    qin, tin, ts, tall, qs, qr, qb, wown, wp, wps, wt, hown, hv, hs, qwb, qwbb, sbuf, psum, prec, bo, via,
    in_sem, own_sem, t_send, t_recv, q_send, q_recv, y_send, y_recv, s2_send, s2_recv, s1_send, s1_recv,
    w_send, w_recv, m_send, m_recv, p_send, p_recv, v_send, v_recv,
):
    n_db = lax.axis_size("db")
    db = lax.axis_index("db")
    pb = lax.axis_index("pb")
    z = pb // 2
    yh = lax.rem(pb, 2)
    core = lax.rem(db, 2)
    mate = db + 1 - 2 * core
    last_x = lax.rem(db, 8) >= 6
    first_x = lax.rem(db, 8) < 2
    depth = ts.shape[2]
    half = qs.shape[3]

    def zdev(k):
        return (db, k * 2 + yh)

    def step_of(j):
        far = NZ // 2 - (j + 1) // 2
        return jnp.where(lax.rem(j, 2) == 0, far, NZ - far)

    def to(j):
        return lax.rem(z + step_of(j), NZ)

    def frm(j):
        return lax.rem(z - step_of(j) + NZ, NZ)

    y_dev = (db, pb + 1 - 2 * yh)
    core_dev = (mate, pb)

    def shifted(by):
        return (lax.rem(db + by + n_db, n_db), pb)

    def remote(src, dst, send, recv, dev):
        return pltpu.make_async_remote_copy(
            src_ref=src, dst_ref=dst, send_sem=send, recv_sem=recv, device_id=dev, device_id_type=MESH
        )

    t_loads = [pltpu.make_async_copy(t_hbm.at[b], tin.at[b], in_sem.at[b]) for b in range(8)]
    q_loads = [pltpu.make_async_copy(q_hbm.at[k], qin.at[k], in_sem.at[8 + k]) for k in range(2)]
    for copy in t_loads[:EACH]:
        copy.start()

    barrier = pltpu.get_barrier_semaphore()

    def greet(j, _):
        pl.semaphore_signal(barrier, inc=1, device_id=zdev(frm(j)), device_id_type=MESH)
        return 0

    lax.fori_loop(0, PEERS, greet, 0)
    for dev in (y_dev, core_dev, shifted(-1), shifted(-2)):
        pl.semaphore_signal(barrier, inc=1, device_id=dev, device_id_type=MESH)

    @pl.when(last_x)
    def _():
        pl.semaphore_signal(barrier, inc=1, device_id=shifted(8), device_id_type=MESH)

    @pl.when(first_x)
    def _():
        pl.semaphore_signal(barrier, inc=1, device_id=shifted(-10), device_id_type=MESH)

    flip = (
        lax.broadcasted_iota(jnp.int32, (LANES, LANES), 0) + lax.broadcasted_iota(jnp.int32, (LANES, LANES), 1)
        == LANES - 1
    ).astype(jnp.float32).astype(jnp.bfloat16)
    def turn_targets(g):
        for b in range(EACH):
            turned = jnp.dot(tin[EACH * g + b].T, flip, preferred_element_type=jnp.float32).astype(jnp.bfloat16)
            ts[:, EACH * g + b] = turned.reshape(NZ, depth, LANES)

    def t_copy(g, j):
        k = to(j)
        return remote(
            ts.at[k, pl.ds(EACH * g, EACH)], tall.at[z, pl.ds(EACH * g, EACH)], t_send.at[g, j], t_recv.at[g, j], zdev(k)
        )

    def start_targets(g):
        def go(j, _):
            t_copy(g, j).start()
            return 0

        lax.fori_loop(0, PEERS, go, 0)

    for copy in t_loads[:EACH]:
        copy.wait()
    for copy in t_loads[EACH:] + q_loads:
        copy.start()
    turn_targets(0)
    pl.semaphore_wait(barrier, PEERS + 4 + jnp.where(last_x, 2, 0))

    start_targets(0)

    position = lax.broadcasted_iota(jnp.int32, (8, LANES), 1)
    place = lax.broadcasted_iota(jnp.int32, (8, LANES), 0)
    lengths = jnp.zeros((8, LANES), jnp.int32)
    for b in range(8):
        lengths = jnp.where(place == b, tln[b], lengths)
    t_scale = tsc[...].astype(jnp.float32)
    t_weight = jnp.where(tmk[...] == 1, jnp.where(position < lengths, t_scale, 0.0), 0.0)
    t_weight = jnp.dot(t_weight.astype(jnp.bfloat16), flip, preferred_element_type=jnp.float32)
    q_scale = qsc[...].astype(jnp.float32)
    q_mask = qmk[...]
    q_rows = []
    for k in range(2):
        for m in range(4):
            cols = slice(m * LANES, (m + 1) * LANES)
            at = lax.broadcasted_iota(jnp.int32, (1, LANES), 1) + m * LANES
            kept = jnp.where(at < qln[k], q_scale[k : k + 1, cols], 0.0)
            q_rows.append(jnp.where(q_mask[k : k + 1, cols] == 1, kept, 0.0))
    wown[...] = jnp.concatenate([t_weight] + q_rows, axis=0).astype(jnp.bfloat16)
    hown[...] = jnp.concatenate([h_in[0:1], h_in[1:2], jnp.zeros((1, LANES - 16), jnp.int32)], axis=1)

    shift_w = [remote(wown, wps.at[i], m_send.at[i], m_recv.at[i], shifted(i + 1)) for i in range(2)]
    for copy in shift_w:
        copy.start()

    def small(j):
        dev = zdev(to(j))
        return [
            remote(wown, wp.at[z], w_send.at[0, j], w_recv.at[0, j], dev),
            remote(hown, hv.at[z], w_send.at[1, j], w_recv.at[1, j], dev),
        ]

    def start_small(j, _):
        for copy in small(j):
            copy.start()
        return 0

    lax.fori_loop(0, PEERS, start_small, 0)
    own_small = [
        pltpu.make_async_copy(wown, wp.at[z], own_sem.at[0]),
        pltpu.make_async_copy(hown, hv.at[z], own_sem.at[1]),
    ]
    for copy in own_small:
        copy.start()

    s2 = [remote(q_hbm.at[k], qb.at[1, k], s2_send.at[k], s2_recv.at[k], shifted(2)) for k in range(2)]
    s1_even = [remote(q_hbm.at[k], qb.at[0, k], s1_send.at[k], s1_recv.at[k], core_dev) for k in range(2)]
    s1_odd = [remote(qb.at[1, k], qb.at[0, k], s1_send.at[k], s1_recv.at[k], core_dev) for k in range(2)]
    s2_first = remote(q_hbm.at[1], via, v_send.at[0], v_recv.at[0], shifted(8))
    s2_then = remote(via, qb.at[1, 1], s2_send.at[1], s2_recv.at[1], shifted(10))
    s2[0].start()

    @pl.when(last_x)
    def _():
        s2_first.start()

    @pl.when(jnp.logical_not(last_x))
    def _():
        s2[1].start()

    @pl.when(core == 0)
    def _():
        for copy in s1_even:
            copy.start()

    for copy in t_loads[EACH:]:
        copy.wait()

    def send_targets(g, _):
        turn_targets(g)

        @pl.when(g < AHEAD)
        def _():
            start_targets(g)

        return 0

    lax.fori_loop(1, GROUPS, send_targets, 0)
    own_t = pltpu.make_async_copy(ts.at[z], tall.at[z], own_sem.at[3])
    own_t.start()

    for copy in q_loads:
        copy.wait()

    def q_copy(c, j):
        k = to(j)
        return remote(qs.at[k, c], qr.at[z, c], q_send.at[c, j], q_recv.at[c, j], zdev(k))

    def start_chunk(c):
        def go(j, _):
            q_copy(c, j).start()
            return 0

        lax.fori_loop(0, PEERS, go, 0)

    def turn_queries(c, _):
        rows = pl.ds(pl.multiple_of(lax.rem(c, 2) * half, half), half)
        turned = qin[c // 2, rows, :].T
        qs[:, c] = turned.reshape(NZ, depth, half)

        @pl.when(c + GROUPS < AHEAD)
        def _():
            start_chunk(c)

        return 0

    lax.fori_loop(0, CHUNKS, turn_queries, 0)
    own_q = pltpu.make_async_copy(qs.at[z], qr.at[z], own_sem.at[4])
    own_q.start()

    def y_copy(g, i, src):
        part = pl.ds(EACH * g, EACH)
        return remote(tall.at[src, part], tall.at[NZ + src, part], y_send.at[g, i], y_recv.at[g, i], y_dev)

    own_t.wait()

    def pass_on(g, _):
        y_copy(g, PEERS, z).start()

        def go(j, _):
            t_copy(g, j).wait_recv()
            y_copy(g, j, frm(j)).start()
            later = g + AHEAD

            @pl.when(later < GROUPS)
            def _():
                t_copy(later, j).start()

            @pl.when(jnp.logical_and(later >= GROUPS, later < GROUPS + CHUNKS))
            def _():
                q_copy(later - GROUPS, j).start()

            return 0

        lax.fori_loop(0, PEERS, go, 0)

        @pl.when(jnp.logical_and(g == 0, last_x))
        def _():
            s2_first.wait()
            s2_then.start()

        return 0

    lax.fori_loop(0, GROUPS, pass_on, 0)

    def wait_small(j, _):
        for copy in small(j):
            copy.wait()
        return 0

    lax.fori_loop(0, PEERS, wait_small, 0)
    for copy in own_small:
        copy.wait()
    to_scalars = pltpu.make_async_copy(hv, hs, own_sem.at[5])
    to_scalars.start()
    for copy in shift_w:
        copy.wait()
    y_small = remote(wp.at[pl.ds(0, NZ)], wp.at[pl.ds(NZ, NZ)], m_send.at[2], m_recv.at[2], y_dev)
    y_small.start()

    def spread(row):
        return jnp.broadcast_to(row, (LANES, LANES)).T

    def spread_all(i, _):
        w = wp[i].astype(jnp.float32)
        for m in range(8):
            rows = pl.ds((m % 4) * LANES, LANES)
            qwb[2 * i + m // 4, rows, :] = spread(w[8 + m : 9 + m])
        return 0

    lax.fori_loop(0, NZ, spread_all, 0)

    def widen(o, _):
        w = wp[o].astype(jnp.float32)
        for b in range(8):
            wt[o, b] = jnp.broadcast_to(w[b : b + 1], (8, LANES))
        return 0

    lax.fori_loop(0, NZ, widen, 0)

    def spread_shift(i, _):
        w = wps[i].astype(jnp.float32)
        for m in range(8):
            rows = pl.ds((m % 4) * LANES, LANES)
            qwbb[2 * i + m // 4, rows, :] = spread(w[8 + m : 9 + m])
        return 0

    lax.fori_loop(0, 2, spread_shift, 0)

    def chunk_arrived(c):
        def go(j, _):
            q_copy(c, j).wait_recv()
            later = c + AHEAD

            @pl.when(later < CHUNKS)
            def _():
                q_copy(later, j).start()

            return 0

        lax.fori_loop(0, PEERS, go, 0)

    chunk_arrived(0)

    low = lax.broadcasted_iota(jnp.int32, (LANES, LANES), 1) >= lax.broadcasted_iota(jnp.int32, (LANES, LANES), 0)

    def diagonals(x):
        y = pltpu.roll(x, 0, 1, stride=1, stride_axis=0)
        lower = jnp.where(low, y, 0.0).reshape(LANES // 8, 8, LANES)
        upper = jnp.where(low, 0.0, y).reshape(LANES // 8, 8, LANES)
        return jnp.sum(lower, axis=0), jnp.sum(upper, axis=0)

    def row_sum(v):
        return jnp.sum(v, axis=0, keepdims=True)

    for k in range(2):
        s2[k].wait_recv()

    @pl.when(core == 1)
    def _():
        for copy in s1_odd:
            copy.start()

    def bands(s, k):
        def pair(p, _):
            rhs = jnp.concatenate(
                [ts[:, 2 * p].reshape(NZ * depth, LANES), ts[:, 2 * p + 1].reshape(NZ * depth, LANES)], axis=1
            )
            sbuf[...] = jnp.dot(qb[s, k], rhs, preferred_element_type=jnp.float32)
            for u in range(2):
                w8 = wt[z, 2 * p + u]
                wrow = jnp.broadcast_to(w8[None], (LANES // 8, 8, LANES)).reshape(LANES, LANES)
                row = (s * 8 + 2 * p + u) * 2 + k
                carry = jnp.zeros((8, LANES), jnp.float32)
                for m in range(4):
                    rows = pl.ds(m * LANES, LANES)
                    x = sbuf[rows, u * LANES : (u + 1) * LANES] * qwbb[2 * s + k, rows, :] * wrow
                    lower, upper = diagonals(x)
                    bo[m, pl.ds(row, 1), :] = row_sum(carry + lower)
                    carry = upper
                bo[4, pl.ds(row, 1), :] = row_sum(carry)
            return 0

        lax.fori_loop(0, 4, pair, 0)

    lax.fori_loop(0, 2, lambda k, c: (bands(1, k), c)[1], 0)
    chunk_arrived(1)
    for k in range(2):
        s1_even[k].wait_recv()
    lax.fori_loop(0, 2, lambda k, c: (bands(0, k), c)[1], 0)

    def scores(segments):
        g = jnp.concatenate(segments, axis=1)
        return g + pltpu.roll(g, 1, 1)

    band = scores([bo[m] for m in range(5)])
    for s in range(2):
        for t in range(8):
            band_ref[s, t] = band[(s * 8 + t) * 2 : (s * 8 + t) * 2 + 2]

    own_q.wait()
    to_scalars.wait()
    y_small.wait()
    lax.fori_loop(NZ, 2 * NZ, widen, 0)
    psum[...] = jnp.zeros_like(psum)

    def wait_y(g, _):
        def go(j, _):
            y_copy(g, j, frm(j)).wait()
            return 0

        lax.fori_loop(0, PEERS, go, 0)
        y_copy(g, PEERS, z).wait()
        return 0

    lax.fori_loop(0, GROUPS, wait_y, 0)

    def p_copy(part, j):
        k = to(j)
        tile, seg, count = ((0, 0, 5), (1, 0, 2), (1, 2, 3))[part]
        return remote(
            psum.at[k, tile, pl.ds(seg, count)], prec.at[z, tile, pl.ds(seg, count)],
            p_send.at[part, j], p_recv.at[part, j], zdev(k),
        )

    def start_p(part):
        def go(j, _):
            p_copy(part, j).start()
            return 0

        lax.fori_loop(0, PEERS, go, 0)

    def chunk(c, _):
        @pl.when(c >= 2)
        def _():
            chunk_arrived(c)

        @pl.when(c == CHUNKS - 1)
        def _():
            start_p(0)
            start_p(1)

        tile, part = c // 2, lax.rem(c, 2)
        first = pl.multiple_of(part * half, half)

        def query(zq, _):
            lhs = qr[zq, c].T
            for pair in range(4):
                where = []
                for u in range(2):
                    hit = lax.rem(hs[zq, 0, tile * 8 + 2 * pair + u], 2 * NZ * 8)
                    owner, block = hit // 8, lax.rem(hit, 8)
                    other = jnp.where(lax.rem(owner, 2) == yh, 0, NZ)
                    where.append((other + owner // 2, block))
                rhs = jnp.concatenate([tall[o, b] for o, b in where], axis=1)
                s = jnp.dot(lhs, rhs, preferred_element_type=jnp.float32)
                for u in range(2):
                    o, b = where[u]
                    wrow = jnp.broadcast_to(wt[o, b][None], (LANES // 8, 8, LANES)).reshape(LANES, LANES)
                    row = 2 * pair + u
                    carry = jnp.zeros((8, LANES), jnp.float32)
                    for m in range(2):
                        weight = qwb[2 * zq + tile, pl.ds(first + m * LANES, LANES), :]
                        x = s[m * LANES : (m + 1) * LANES, u * LANES : (u + 1) * LANES] * weight * wrow
                        lower, upper = diagonals(x)
                        psum[zq, tile, 2 * part + m, row : row + 1, :] += row_sum(carry + lower)
                        carry = upper
                    psum[zq, tile, 2 * part + 2, row : row + 1, :] += row_sum(carry)
            return 0

        lax.fori_loop(0, NZ, query, 0)
        return 0

    lax.fori_loop(0, CHUNKS, chunk, 0)

    start_p(2)
    prec[z] = psum[z]

    def sent(j, _):
        for g in range(GROUPS):
            t_copy(g, j).wait_send()
        for c in range(CHUNKS):
            q_copy(c, j).wait_send()
        return 0

    lax.fori_loop(0, PEERS, sent, 0)
    for k in range(2):
        s2[k].wait_send()
        s1_even[k].wait_send()

    def wait_p(j, _):
        for part in range(3):
            p_copy(part, j).wait()
        return 0

    lax.fori_loop(0, PEERS, wait_p, 0)
    total = prec[0]
    for k in range(1, NZ):
        total = total + prec[k]
    for tile in range(2):
        b = scores([total[tile, m] for m in range(5)])
        mean = jnp.sum(jnp.maximum(b, 0.0), axis=1, keepdims=True) / (5 * LANES)
        line = jnp.sum(jnp.where(position == place, jnp.broadcast_to(mean, (8, LANES)), 0.0), axis=0, keepdims=True)
        resc_ref[tile : tile + 1, :] = line[:, 0:8]


def shards(queries, query_scale, query_mask, query_len, targets, target_scale, target_mask, target_len, hit_ids):
    tiles, rows, width = queries.shape
    blocks, cols, _ = targets.shape
    hits = hit_ids.shape[1]
    depth = width // NZ
    half = rows // 2
    vmem = pltpu.VMEM
    one = (pl.ANY, vmem, vmem, pltpu.SMEM)
    spaces = one + one + (vmem,)
    dma = pltpu.SemaphoreType.DMA
    bf, f32 = jnp.bfloat16, jnp.float32
    band, resc = pl.pallas_call(
        kernel,
        out_shape=(
            jax.ShapeDtypeStruct((2, blocks, tiles, rows + cols), f32),
            jax.ShapeDtypeStruct((tiles, hits), f32),
        ),
        in_specs=[pl.BlockSpec(memory_space=m) for m in spaces],
        out_specs=(pl.BlockSpec(memory_space=pltpu.VMEM),) * 2,
        scratch_shapes=[
            vmem((tiles, rows, width), bf),
            vmem((blocks, cols, width), bf),
            vmem((NZ, blocks, depth, cols), bf),
            vmem((2 * NZ, blocks, depth, cols), bf),
            vmem((NZ, CHUNKS, depth, half), bf),
            vmem((NZ, CHUNKS, depth, half), bf),
            vmem((2, tiles, rows, width), bf),
            vmem((16, LANES), bf),
            vmem((2 * NZ, 16, LANES), bf),
            vmem((2, 16, LANES), bf),
            vmem((2 * NZ, blocks, 8, cols), f32),
            vmem((1, LANES), jnp.int32),
            vmem((NZ, 1, LANES), jnp.int32),
            pltpu.SMEM((NZ, 1, LANES), jnp.int32),
            vmem((NZ * tiles, rows, LANES), f32),
            vmem((2 * tiles, rows, LANES), f32),
            vmem((rows, 2 * LANES), f32),
            vmem((NZ, tiles, 5, hits, LANES), f32),
            vmem((NZ, tiles, 5, hits, LANES), f32),
            vmem((5, 2 * blocks * tiles, LANES), f32),
            vmem((rows, width), bf),
            dma((10,)),
            dma((6,)),
            dma((GROUPS, PEERS)), dma((GROUPS, PEERS)),
            dma((CHUNKS, PEERS)), dma((CHUNKS, PEERS)),
            dma((GROUPS, NZ)), dma((GROUPS, NZ)),
            dma((2,)), dma((2,)),
            dma((2,)), dma((2,)),
            dma((2, PEERS)), dma((2, PEERS)),
            dma((3,)), dma((3,)),
            dma((3, PEERS)), dma((3, PEERS)),
            dma((1,)), dma((1,)),
        ],
        compiler_params=pltpu.CompilerParams(
            collective_id=0, has_side_effects=True, vmem_limit_bytes=56 * 1024 * 1024
        ),
    )(queries, query_scale, query_mask, query_len, targets, target_scale, target_mask, target_len, hit_ids)
    return band, resc


def solution(mesh):
    in_specs = (
        P(("db", "pb"), None, None),
        P(("db", "pb"), None),
        P(("db", "pb"), None),
        P(("db", "pb")),
        P(("db", "pb"), None, None),
        P(("db", "pb"), None),
        P(("db", "pb"), None),
        P(("db", "pb")),
        P(("db", "pb"), None),
    )
    out_specs = (P(None, ("db", "pb"), None, None), P(("db", "pb"), None))
    return jax.shard_map(shards, mesh=mesh, in_specs=in_specs, out_specs=out_specs, check_vma=False)
```
